256 devices in a mesh: gx: 64 (over z, x, core), gy: 4 (over y).
Axes of the slice: x: 4, y: 4, z: 8, core: 2. Of those that a mesh axis runs over, the one named last changes fastest.
Arguments:
- velocity: float32 [3, 256, 64, 256], P(None, 'gx', 'gy')
- cell_swimmer: int32 [256, 64, 256], P('gx', 'gy'), may hold values from 0 to 15, as said below
- swimmer_speed: float32 [8, 3], replicated, may hold values from -1 to 1
- recentre_cols: int32 [2], replicated, may hold values from 0 to 2, as said below
Outputs:
- velocity_out: float32 [3, 256, 64, 256], P(None, 'gx', 'gy')
- pressure: float32 [256, 64, 256], P('gx', 'gy')
The draws below stay inside these ranges and needn't reach their ends.
Inputs may be any that keep to these rules, and one draw needn't show every extreme that they name: `cell_swimmer`: values of 8 or more mark fluid cells, smaller ones name the swimmer; the cells of each swimmer lie inside one box of 8 by 8 by 32 cells, periodic along the first and third dimensions. `recentre_cols`: some step recentres by exactly 2 columns.
All inputs are finite; a program needn't handle non-finite values.
Results may differ from the reference program's by a relative error of at most 0.0003.
Values sent between devices are 32-bit elements; how exact they have to be, the bound alone decides.
No kernel may reach another device: no remote copies, remote signals or barrier semaphores. Data moves between devices by JAX's collectives and lax.ppermute only.
A program may use at most 64 MiB of HBM per device.

```python
import math
import jax
import jax.numpy as jnp
from jax import lax

CX = 4
CY = 16
NZ = 256
SWIMMERS = 8
STEPS = 2
PASSES = 8
SMAX = 2
NX = 256
NY = 64


def smooth_modes(key, amplitude):
    phases = jax.random.uniform(key, (3, 4), jnp.float32, 0.0, 2.0 * math.pi)
    rows_x = (jnp.arange(NX, dtype=jnp.float32) / NX)[:, None, None]
    rows_y = jnp.arange(NY, dtype=jnp.float32)[None, :, None]
    rows_z = (jnp.arange(NZ, dtype=jnp.float32) / NZ)[None, None, :]
    wave_x = float(max(1, NX // 16))
    wave_z = float(max(1, NZ // 16))
    half_rows = NY // 2
    profile = jnp.sin(math.pi * (rows_y + 1.0) / (half_rows + 1.0)) * (rows_y < half_rows).astype(jnp.float32)
    components = []
    for component in range(3):
        leading = jnp.sin(2.0 * math.pi * wave_x * rows_x + phases[component, 0]) * jnp.cos(2.0 * math.pi * wave_z * rows_z + phases[component, 1])
        trailing = 0.5 * jnp.sin(4.0 * math.pi * wave_x * rows_x + phases[component, 2]) * jnp.sin(4.0 * math.pi * wave_z * rows_z + phases[component, 3])
        components.append((leading + trailing) * profile)
    return amplitude * jnp.stack(components)


def draw_velocity(key, part):
    key = jax.random.fold_in(key, 3)
    key_one = jax.random.fold_in(key, 0)
    key_three = jax.random.fold_in(key, 2)
    position = (jnp.arange(NX, dtype=jnp.float32) / NX)[None, :, None, None]
    sweep = 0.5 + 1.5 * position
    span_rows = jnp.arange(NY, dtype=jnp.float32)[None, None, :, None]
    noisy_rows = (span_rows >= NY // 2).astype(jnp.float32)
    noise = jax.random.normal(key_one, (3, NX, NY, NZ), jnp.float32)
    return (noise * sweep * noisy_rows + smooth_modes(key_three, 1.5)).astype(jnp.float32)


def draw_cell_swimmer(key, part):
    key = jax.random.fold_in(key, 7)
    key_fluid, key_x, key_y, key_z = jax.random.split(key, 4)
    cells = jax.random.randint(key_fluid, (NX, NY, NZ), SWIMMERS, 2 * SWIMMERS)
    box_x = 2 * CX
    box_y = max(1, CY // 2)
    box_z = max(1, NZ // 8)
    starts_x = jax.random.randint(key_x, (SWIMMERS,), 0, NX)
    starts_y = jax.random.randint(key_y, (SWIMMERS,), 0, NY - box_y + 1)
    starts_z = jax.random.randint(key_z, (SWIMMERS,), 0, NZ)
    index_x = jnp.arange(NX, dtype=jnp.int32)[:, None, None]
    index_y = jnp.arange(NY, dtype=jnp.int32)[None, :, None]
    index_z = jnp.arange(NZ, dtype=jnp.int32)[None, None, :]
    for swimmer in reversed(range(SWIMMERS)):
        inside_x = jnp.mod(index_x - starts_x[swimmer], NX) < box_x
        offset_y = index_y - starts_y[swimmer]
        inside_y = (offset_y >= 0) & (offset_y < box_y)
        inside_z = jnp.mod(index_z - starts_z[swimmer], NZ) < box_z
        cells = jnp.where(inside_x & inside_y & inside_z, swimmer, cells)
    return cells.astype(jnp.int32)


def draw_recentre_cols(key, part):
    key = jax.random.fold_in(key, 5)
    key_one, key_two = jax.random.split(key)
    values = jax.random.randint(key_one, (STEPS,), 0, SMAX + 1)
    chosen = jax.random.randint(key_two, (), 0, STEPS)
    return jnp.where(jnp.arange(STEPS) == chosen, SMAX, values).astype(jnp.int32)


def setup_inputs(seed: int = 0) -> dict:
    key_of = jax.random.split(jax.random.key(seed), 5)
    return {
        "velocity": draw_velocity(jax.random.fold_in(key_of[4], 71), 0),
        "cell_swimmer": draw_cell_swimmer(jax.random.fold_in(key_of[4], 71), 0),
        "swimmer_speed": jnp.clip(jax.random.uniform(key_of[2], (SWIMMERS, 3), jnp.float32, -1.0, 1.0), -1.0, 1.0),
        "recentre_cols": draw_recentre_cols(jax.random.fold_in(key_of[4], 71), 0),
    }


TIME_STEP = 0.1
VISCOSITY = 0.5
PENALTY = 4.0
SCREEN = 0.05


def pad_field(field, width):
    lead = [(0, 0)] * (field.ndim - 3)
    wrapped = jnp.pad(field, lead + [(width, width), (0, 0), (0, 0)], mode="wrap")
    return jnp.pad(wrapped, lead + [(0, 0), (width, width), (0, 0)])


def neighbours(padded):
    centre = padded[..., 1:-1, 1:-1, :]
    x_plus = padded[..., 2:, 1:-1, :]
    x_minus = padded[..., :-2, 1:-1, :]
    y_plus = padded[..., 1:-1, 2:, :]
    y_minus = padded[..., 1:-1, :-2, :]
    z_plus = jnp.roll(centre, -1, axis=-1)
    z_minus = jnp.roll(centre, 1, axis=-1)
    return centre, x_plus, x_minus, y_plus, y_minus, z_plus, z_minus


def operate(padded):
    centre, x_plus, x_minus, y_plus, y_minus, z_plus, z_minus = neighbours(padded)
    return (6.0 + SCREEN) * centre - (x_plus + x_minus + y_plus + y_minus + z_plus + z_minus)


def advect(padded):
    centre, x_plus, x_minus, y_plus, y_minus, z_plus, z_minus = neighbours(padded)
    laplace = x_plus + x_minus + y_plus + y_minus + z_plus + z_minus - 6.0 * centre
    transport = centre[0:1] * (x_plus - x_minus) * 0.5 + centre[1:2] * (y_plus - y_minus) * 0.5 + centre[2:3] * (z_plus - z_minus) * 0.5
    return centre + TIME_STEP * (VISCOSITY * laplace - transport)


def penalize(velocity, cell_swimmer, swimmer_speed):
    target = jnp.zeros_like(velocity)
    for swimmer in range(SWIMMERS):
        target = target + (cell_swimmer == swimmer).astype(jnp.float32)[None] * swimmer_speed[swimmer][:, None, None, None]
    solid = (cell_swimmer < SWIMMERS).astype(jnp.float32)[None]
    return (velocity + PENALTY * solid * target) / (1.0 + PENALTY * solid)


def divergence(flux_x, flux_y, flux_z):
    return (flux_x[2:] - flux_x[:-2]) * 0.5 + (flux_y[:, 2:] - flux_y[:, :-2]) * 0.5 + (jnp.roll(flux_z, -1, axis=2) - jnp.roll(flux_z, 1, axis=2)) * 0.5


def gradient(padded):
    centre, x_plus, x_minus, y_plus, y_minus, z_plus, z_minus = neighbours(padded)
    return jnp.stack([(x_plus - x_minus) * 0.5, (y_plus - y_minus) * 0.5, (z_plus - z_minus) * 0.5])


def reference(velocity, cell_swimmer, swimmer_speed, recentre_cols):
    pressure = jnp.zeros(velocity.shape[1:], jnp.float32)
    for step_index in range(STEPS):
        offset = recentre_cols[step_index].astype(jnp.int32)
        joined = jnp.concatenate([velocity[:, NX - SMAX:], velocity], axis=1)
        velocity = lax.dynamic_slice_in_dim(joined, (SMAX - offset).astype(jnp.int32), NX, 1)
        velocity = advect(pad_field(velocity, 1))
        velocity = penalize(velocity, cell_swimmer, swimmer_speed)
        flux_x = jnp.pad(velocity[0], ((1, 1), (0, 0), (0, 0)), mode="wrap")
        flux_y = jnp.pad(velocity[1], ((0, 0), (1, 1), (0, 0)))
        source = -divergence(flux_x, flux_y, velocity[2])
        pressure = jnp.zeros_like(source)
        residual = source
        for pass_index in range(PASSES):
            image = operate(pad_field(residual, 1))
            norm_sq = jnp.sum(residual * residual)
            curvature = jnp.sum(residual * image)
            alpha = norm_sq / curvature
            pressure = pressure + alpha * residual
            residual = residual - alpha * image
        velocity = velocity - gradient(pad_field(pressure, 1))
    return velocity, pressure
```

```python
import functools

import jax
import jax.numpy as jnp
import numpy as np
from jax import lax
from jax.experimental import pallas as pl
from jax.experimental.pallas import tpu as pltpu
from jax.sharding import PartitionSpec as P

SWIMMERS = 8
STEPS = 2
PASSES = 8
SMAX = 2

TIME_STEP = 0.1
VISCOSITY = 0.5
PENALTY = 4.0
SCREEN = 0.05

AXES = ("gx", "gy")
NODES = 16
NZ = 256
DEPTH = 8
NOISE = 1e-4


def shifted(value, axis, steps):
    count = lax.axis_size(axis)
    pairs = [(source, (source + steps) % count) for source in range(count)]
    return lax.ppermute(value, axis, pairs)


def padded_2(cells, sides, width, closed):
    for axis, dim in sides:
        count = lax.axis_size(axis)
        ends = count if closed else count - 1
        head = lax.slice_in_dim(cells, 0, width, axis=dim)
        tail = lax.slice_in_dim(cells, cells.shape[dim] - width, cells.shape[dim], axis=dim)
        cells = jnp.concatenate(
            [
                lax.ppermute(tail, axis, [(i, (i + 1) % count) for i in range(ends)]),
                cells,
                lax.ppermute(head, axis, [((i + 1) % count, i) for i in range(ends)]),
            ],
            axis=dim,
        )
    return cells


def pad_walls(padded, width):
    row_count = padded.shape[-2]
    inner_rows = row_count - 2 * width
    global_rows = lax.axis_index("gy") * inner_rows + jnp.arange(row_count, dtype=jnp.int32) - width
    total_rows = inner_rows * lax.axis_size("gy")
    inside = ((global_rows >= 0) & (global_rows < total_rows)).astype(padded.dtype)
    return padded * inside[:, None]


def neighbours(padded):
    centre = padded[..., 1:-1, 1:-1, :]
    x_plus = padded[..., 2:, 1:-1, :]
    x_minus = padded[..., :-2, 1:-1, :]
    y_plus = padded[..., 1:-1, 2:, :]
    y_minus = padded[..., 1:-1, :-2, :]
    z_plus = jnp.roll(centre, -1, axis=-1)
    z_minus = jnp.roll(centre, 1, axis=-1)
    return (centre, x_plus, x_minus, y_plus, y_minus, z_plus, z_minus)


def operate(padded):
    centre, x_plus, x_minus, y_plus, y_minus, z_plus, z_minus = neighbours(padded)
    return (6.0 + SCREEN) * centre - (x_plus + x_minus + y_plus + y_minus + z_plus + z_minus)


def advect(padded):
    centre, x_plus, x_minus, y_plus, y_minus, z_plus, z_minus = neighbours(padded)
    laplace = x_plus + x_minus + y_plus + y_minus + z_plus + z_minus - 6.0 * centre
    transport = (
        centre[0:1] * (x_plus - x_minus) * 0.5
        + centre[1:2] * (y_plus - y_minus) * 0.5
        + centre[2:3] * (z_plus - z_minus) * 0.5
    )
    return centre + TIME_STEP * (VISCOSITY * laplace - transport)


def penalize(velocity, cell_swimmer, swimmer_speed):
    target = jnp.zeros_like(velocity)
    for swimmer in range(SWIMMERS):
        target = (
            target
            + (cell_swimmer == swimmer).astype(jnp.float32)[None]
            * swimmer_speed[swimmer][:, None, None, None]
        )
    solid = (cell_swimmer < SWIMMERS).astype(jnp.float32)[None]
    return (velocity + PENALTY * solid * target) / (1.0 + PENALTY * solid)


def divergence(flux_x, flux_y, flux_z):
    return (
        (flux_x[2:] - flux_x[:-2]) * 0.5
        + (flux_y[:, 2:] - flux_y[:, :-2]) * 0.5
        + (jnp.roll(flux_z, -1, axis=2) - jnp.roll(flux_z, 1, axis=2)) * 0.5
    )


def gradient(padded):
    centre, x_plus, x_minus, y_plus, y_minus, z_plus, z_minus = neighbours(padded)
    return jnp.stack([(x_plus - x_minus) * 0.5, (y_plus - y_minus) * 0.5, (z_plus - z_minus) * 0.5])


def plain(velocity, cell_swimmer, swimmer_speed, recentre_cols):
    width_x = velocity.shape[1]

    def search(_, state):
        pressure, residual = state
        extended = pad_walls(padded_2(residual, (("gx", 0), ("gy", 1)), 1, True), 1)
        image = operate(extended)
        norm_sq, curvature = lax.psum((jnp.sum(residual * residual), jnp.sum(residual * image)), AXES)
        alpha = norm_sq / curvature
        return (pressure + alpha * residual, residual - alpha * image)

    def step(step_index, state):
        velocity, _ = state
        offset = recentre_cols[step_index]
        tail_cols = velocity[:, width_x - SMAX :]
        received = shifted(tail_cols, "gx", 1)
        joined = jnp.concatenate([received, velocity], axis=1)
        velocity = lax.dynamic_slice_in_dim(joined, SMAX - offset, width_x, 1)
        padded = pad_walls(padded_2(velocity, (("gx", 1), ("gy", 2)), 1, True), 1)
        velocity = advect(padded)
        velocity = penalize(velocity, cell_swimmer, swimmer_speed)
        flux_x = padded_2(velocity[0], (("gx", 0),), 1, True)
        flux_y = padded_2(velocity[1], (("gy", 1),), 1, False)
        source = -divergence(flux_x, flux_y, velocity[2])
        pressure, _ = lax.fori_loop(0, PASSES, search, (jnp.zeros_like(source), source))
        padded = pad_walls(padded_2(pressure, (("gx", 0), ("gy", 1)), 1, True), 1)
        return (velocity - gradient(padded), pressure)

    start = (velocity, jnp.zeros(velocity.shape[1:], jnp.float32))
    return lax.fori_loop(0, STEPS, step, start)


def tables():
    angle = (np.arange(NODES) + 0.5) * np.pi / NODES
    cheb = np.cos(np.outer(np.arange(NODES), angle))
    moment = np.zeros((NODES, NODES))
    moment[0, 0] = moment[1, 1] = 1.0
    for i in range(1, NODES // 2):
        moment[2 * i, 2 * i], moment[2 * i, 0] = 2.0, -1.0
        moment[2 * i + 1, 2 * i + 1], moment[2 * i + 1, 1] = 2.0, -1.0
    scale = np.full((NODES, 1), 2.0 / NODES)
    scale[0] = 1.0 / NODES
    weight = cheb.T @ (scale * moment)
    weight_map = np.zeros((NODES, 128))
    weight_map[:, :NODES] = weight
    node = (6.0 + SCREEN) - 6.0 * np.cos(angle)
    node = np.broadcast_to(node[:, None], (NODES, NZ))
    coef = np.broadcast_to((scale * cheb)[:PASSES, :, None], (PASSES, NODES, NZ))
    return [np.ascontiguousarray(a, dtype=np.float32) for a in (weight_map, node, coef)]


def z_next(a):
    return pltpu.roll(a, NZ - 1, a.ndim - 1)


def z_prev(a):
    return pltpu.roll(a, 1, a.ndim - 1)


def y_next(a):
    return pltpu.roll(a, a.shape[0] - 1, 0)


def y_prev(a):
    return pltpu.roll(a, 1, 0)


def window_kernel(info, own, left, right, win, to_core, to_chip):
    core, offset = info[0], info[1]
    joined = 2 - offset

    def plane(i, _):
        j = i + joined
        for c in range(3):

            def put(row):
                win[c, i] = row
                top, bottom = row[0:2], row[6:8]
                to_core[c, i] = jnp.where(core == 0, bottom, top)
                to_chip[c, i] = jnp.where(core == 0, top, bottom)

            @pl.when(j < 4)
            def _():
                put(left[c, j])

            @pl.when((j >= 4) & (j < 12))
            def _():
                put(own[c, j - 4])

            @pl.when(j >= 12)
            def _():
                put(right[c, j - 12])

        return 0

    lax.fori_loop(0, 12, plane, 0)


def source_kernel(info, flags, speed, win, from_core, from_chip, cell, cell_core, cell_chip, bodied, source, pad, body):
    core = info[0]
    rows = lax.broadcasted_iota(jnp.int32, (24, NZ), 0)
    inside = jnp.where(rows < 8, flags[0], jnp.where(rows < 16, 1.0, flags[1]))

    def fill(i, _):
        for c in range(3):
            pad[c, i, 8:16] = win[c, i]
            a, b = from_core[c, i], from_chip[c, i]
            pad[c, i, 6:8] = jnp.where(core == 0, b, a)
            pad[c, i, 16:18] = jnp.where(core == 0, a, b)
        return 0

    lax.fori_loop(0, 12, fill, 0)

    def move(i, _):
        a, b = cell_core[i], cell_chip[i]
        up = jnp.where(core == 0, b, a)
        down = jnp.where(core == 0, a, b)
        ids = jnp.concatenate(
            [jnp.broadcast_to(up, (8, NZ)), cell[i], jnp.broadcast_to(down, (8, NZ))], axis=0
        )
        centre = [pad[c, i + 1] for c in range(3)]
        solid = ids < SWIMMERS
        factor = jnp.where(solid, 1.0 / (1.0 + PENALTY), 1.0) * inside
        for c in range(3):
            x_plus, x_minus = pad[c, i + 2], pad[c, i]
            y_plus, y_minus = y_next(centre[c]), y_prev(centre[c])
            z_plus, z_minus = z_next(centre[c]), z_prev(centre[c])
            laplace = x_plus + x_minus + y_plus + y_minus + z_plus + z_minus - 6.0 * centre[c]
            transport = (
                centre[0] * (x_plus - x_minus)
                + centre[1] * (y_plus - y_minus)
                + centre[2] * (z_plus - z_minus)
            )
            moved = centre[c] + (TIME_STEP * VISCOSITY) * laplace - (TIME_STEP * 0.5) * transport
            target = jnp.zeros((24, NZ), jnp.float32)
            for swimmer in range(SWIMMERS):
                target = jnp.where(ids == swimmer, speed[swimmer, c], target)
            body[c, i] = (moved + PENALTY * target) * factor
        return 0

    lax.fori_loop(0, 10, move, 0)

    def diverge(i, _):
        along_x = body[0, i + 2, 8:16] - body[0, i, 8:16]
        b1 = body[1, i + 1]
        along_y = (y_next(b1) - y_prev(b1))[8:16]
        b2 = body[2, i + 1, 8:16]
        source[i] = -0.5 * (along_x + along_y + z_next(b2) - z_prev(b2))
        for c in range(3):
            bodied[c, i] = body[c, i + 1, 8:16]
        return 0

    lax.fori_loop(0, 8, diverge, 0)


def powers_kernel(info, flags, own, left, right, from_core, from_chip, moments, near, t):
    core = info[0]
    rows = lax.broadcasted_iota(jnp.int32, (24, NZ), 0)
    inside = jnp.where(rows < 8, flags[0], jnp.where(rows < 16, 1.0, flags[1]))
    twice = inside * (1.0 / 3.0)
    once = inside * (1.0 / 6.0)

    def fill(i, _):
        a, b = from_core[i], from_chip[i]
        t[0, i, 0:8] = jnp.where(core == 0, b, a)
        t[0, i, 16:24] = jnp.where(core == 0, a, b)
        return 0

    lax.fori_loop(0, 24, fill, 0)
    for i in range(8):
        t[0, i, 8:16] = left[i]
        t[0, i + 8, 8:16] = own[i]
        t[0, i + 16, 8:16] = right[i]

    for j in range(1, PASSES + 1):

        def level(i, _, j=j):
            centre = t[j - 1, i]
            total = (
                t[j - 1, i - 1]
                + t[j - 1, i + 1]
                + (y_next(centre) + y_prev(centre))
                + (z_next(centre) + z_prev(centre))
            )
            if j == 1:
                t[j, i] = once * total
            else:
                t[j, i] = twice * total - t[j - 2, i]
            return 0

        lax.fori_loop(j, 24 - j, level, 0, unroll=2)

    def product(i, sums):
        values = [t[j, i, 8:16] for j in range(PASSES + 1)]
        out = []
        for j in range(PASSES):
            for k in (j, j + 1):
                both = values[j] * values[k]
                out.append(sums[2 * j + k - j] + (both[:, :128] + both[:, 128:]))
        return tuple(out)

    zero = jnp.zeros((8, 128), jnp.float32)
    sums = lax.fori_loop(DEPTH, 2 * DEPTH, product, (zero,) * NODES)
    lines = [jnp.sum(a, axis=0, keepdims=True) for a in sums]
    block = jnp.concatenate(lines + [jnp.zeros((128 - NODES, 128), jnp.float32)], axis=0)
    line = jnp.sum(block.T, axis=0, keepdims=True)
    moments[...] = jnp.broadcast_to(line, moments.shape)

    def keep(i, _):
        for j in range(PASSES):
            near[j, i] = t[j, i + DEPTH - 1]
        return 0

    lax.fori_loop(0, 10, keep, 0)


def lengths(moments, weight_map, node, coef):
    line = jnp.sum(moments[...], axis=0, keepdims=True)
    weight = jnp.sum(weight_map[...] * line, axis=1, keepdims=True)
    weight = jnp.broadcast_to(weight, (NODES, NZ))
    first = jnp.sum(weight, axis=0, keepdims=True)
    value = node[...]
    residual = jnp.ones((NODES, NZ), jnp.float32)
    search = jnp.zeros((NODES, NZ), jnp.float32)
    good = jnp.ones((1, NZ), jnp.float32)
    for _ in range(PASSES):
        square = residual * residual
        norm_sq = jnp.sum(weight * square, axis=0, keepdims=True)
        curvature = jnp.sum(weight * square * value, axis=0, keepdims=True)
        noise = NOISE * first * jnp.sum(square, axis=0, keepdims=True)
        noise_image = NOISE * first * jnp.sum(square * value, axis=0, keepdims=True)
        good = jnp.where((norm_sq > noise) & (curvature > noise_image), good, 0.0)
        alpha = norm_sq / curvature
        search = search + alpha * residual
        residual = residual - alpha * value * residual
    terms = [jnp.sum(coef[j] * search, axis=0, keepdims=True) for j in range(PASSES)]
    return terms, good


def correct(terms, near, bodied, emit, p):
    def combine(i, _):
        total = terms[0] * near[0, i]
        for j in range(1, PASSES):
            total = total + terms[j] * near[j, i]
        p[i] = total
        return 0

    lax.fori_loop(0, 10, combine, 0)

    def apply(i, _):
        centre = p[i + 1]
        own = centre[8:16]
        emit(
            i,
            bodied[0, i] - 0.5 * (p[i + 2, 8:16] - p[i, 8:16]),
            bodied[1, i] - 0.5 * (y_next(centre) - y_prev(centre))[8:16],
            bodied[2, i] - 0.5 * (z_next(own) - z_prev(own)),
            own,
        )
        return 0

    lax.fori_loop(0, 8, apply, 0)


def inner_step_kernel(moments, weight_map, node, coef, near, bodied, good_out, velocity, p):
    terms, good = lengths(moments, weight_map, node, coef)
    good_out[...] = good

    def emit(i, a, b, c, _):
        velocity[0, i] = a
        velocity[1, i] = b
        velocity[2, i] = c

    correct(terms, near, bodied, emit, p)


def last_step_kernel(info, moments, weight_map, node, coef, near, bodied, good_out, kept, sent, p, fields):
    terms, good = lengths(moments, weight_map, node, coef)
    good_out[...] = good
    core = info[0]

    def emit(i, *values):
        for c in range(4):
            fields[c, i] = values[c]

    correct(terms, near, bodied, emit, p)
    for i in range(4):
        for c in range(4):
            kept[c, i] = fields[c, 4 * core + i]
            sent[c, i] = fields[c, 4 * (1 - core) + i]


SMEM = pl.BlockSpec(memory_space=pltpu.SMEM)
VMEM = pl.BlockSpec(memory_space=pltpu.VMEM)


def call(kernel, args, smem, outs, scratch, flops=1_000_000):
    return pl.pallas_call(
        kernel,
        in_specs=[SMEM] * smem + [VMEM] * (len(args) - smem),
        out_specs=[VMEM] * len(outs),
        out_shape=[jax.ShapeDtypeStruct(s, jnp.float32) for s in outs],
        scratch_shapes=[pltpu.VMEM(s, jnp.float32) for s in scratch],
        compiler_params=pltpu.CompilerParams(vmem_limit_bytes=24 * 1024 * 1024),
        cost_estimate=pl.CostEstimate(flops=flops, bytes_accessed=1_000_000, transcendentals=0),
    )(*args)


def routes(count_x, count_y):
    chips = count_x // 2

    def pairs(target):
        out = []
        for chip in range(chips):
            for core in range(2):
                for y in range(count_y):
                    to = target(chip, core, y)
                    if to is not None:
                        source = (2 * chip + core) * count_y + y
                        out.append((source, (2 * (to[0] % chips) + to[1]) * count_y + to[2]))
        return out

    def across(chip, core, y):
        row = y + (1 if core else -1)
        return (chip, 1 - core, row) if 0 <= row < count_y else None

    return {
        "core": pairs(lambda chip, core, y: (chip, 1 - core, y)),
        "facing": pairs(lambda chip, core, y: (chip + (1 if core else -1), 1 - core, y)),
        "right": pairs(lambda chip, core, y: (chip + 1, core, y)),
        "left": pairs(lambda chip, core, y: (chip - 1, core, y)),
        "across": pairs(across),
    }


def body(velocity, cell_swimmer, swimmer_speed, recentre_cols, *, count_x, count_y):
    route = routes(count_x, count_y)
    send = lambda value, name: lax.ppermute(value, AXES, route[name])
    core = lax.axis_index("gx") % 2
    y = lax.axis_index("gy")
    flags = jnp.stack([(y > 0) | (core == 1), (y < count_y - 1) | (core == 0)]).astype(jnp.float32)
    weight_map, node, coef = (jnp.asarray(a) for a in tables())
    first = core == 0

    cells = cell_swimmer.astype(jnp.float32)
    edge_cells = jnp.where(first, cells[0:1], cells[3:4])
    beside = send(jnp.concatenate([velocity.reshape(12, 16, NZ), edge_cells], axis=0), "facing")
    chunk = jnp.concatenate([velocity.reshape(12, 16, NZ), cells, beside], axis=0)
    mine = jnp.where(first, chunk[:, 0:8], chunk[:, 8:16])
    theirs = send(jnp.where(first, chunk[:, 8:16], chunk[:, 0:8]), "core")
    low = jnp.where(first, mine, theirs)
    high = jnp.where(first, theirs, mine)
    own = jnp.concatenate([low[0:12].reshape(3, 4, 8, NZ), high[0:12].reshape(3, 4, 8, NZ)], axis=1)
    left = low[16:28].reshape(3, 4, 8, NZ)
    right = high[16:28].reshape(3, 4, 8, NZ)[:, 0:2]
    cell = jnp.concatenate([low[28:29], low[12:16], high[12:16], high[28:29]], axis=0)
    cell_edge = cell[:, 0:1], cell[:, 7:8]
    cell_core = send(jnp.where(first, cell_edge[1], cell_edge[0]), "core")
    cell_chip = send(jnp.where(first, cell_edge[0], cell_edge[1]), "across")

    goods = []
    for step in range(STEPS):
        info = jnp.stack([core, recentre_cols[step]]).astype(jnp.int32)
        if step:
            left = send(own[:, 4:8], "right")
            right = send(own[:, 0:2], "left")
        win, to_core, to_chip = call(
            window_kernel,
            (info, own, left, right),
            1,
            [(3, 12, 8, NZ), (3, 12, 2, NZ), (3, 12, 2, NZ)],
            [],
        )
        bodied, source = call(
            source_kernel,
            (info, flags, swimmer_speed, win, send(to_core, "core"), send(to_chip, "across"), cell, cell_core, cell_chip),
            3,
            [(3, 8, 8, NZ), (8, 8, NZ)],
            [(3, 12, 24, NZ), (3, 10, 24, NZ)],
        )
        s_left = send(source, "right")
        s_right = send(source, "left")
        column = jnp.concatenate([s_left, source, s_right], axis=0)
        moments, near = call(
            powers_kernel,
            (info, flags, source, s_left, s_right, send(column, "core"), send(column, "across")),
            2,
            [(count_x * count_y, 128), (PASSES, 10, 24, NZ)],
            [(PASSES + 1, 24, 24, NZ)],
        )
        moments = lax.all_to_all(moments, AXES, 0, 0)
        shared = (moments, weight_map, node, coef, near, bodied)
        if step < STEPS - 1:
            good, own = call(
                inner_step_kernel, shared, 0, [(1, NZ), (3, 8, 8, NZ)], [(10, 24, NZ)]
            )
        else:
            good, kept, sent = call(
                last_step_kernel,
                (info,) + shared,
                1,
                [(1, NZ), (4, 4, 8, NZ), (4, 4, 8, NZ)],
                [(10, 24, NZ), (4, 8, 8, NZ)],
            )
        goods.append(good[0, 0])

    def finish(_):
        got = send(sent, "core")
        fields = jnp.concatenate([jnp.where(first, kept, got), jnp.where(first, got, kept)], axis=2)
        return (fields[0:3], fields[3])

    def again(_):
        return plain(velocity, cell_swimmer, swimmer_speed, recentre_cols)

    return lax.cond(goods[0] * goods[1] > 0.5, finish, again, None)


def solution(mesh):
    placed = (P(None, "gx", "gy", None), P("gx", "gy", None), P(), P())
    return jax.shard_map(
        functools.partial(body, count_x=mesh.shape["gx"], count_y=mesh.shape["gy"]),
        mesh=mesh,
        in_specs=placed,
        out_specs=(P(None, "gx", "gy", None), P("gx", "gy", None)),
        check_vma=False,
    )
```

```python
import functools

import jax
import jax.numpy as jnp
import numpy as np
from jax import lax
from jax.experimental import pallas as pl
from jax.experimental.pallas import tpu as pltpu
from jax.sharding import PartitionSpec as P

SWIMMERS = 8
STEPS = 2
PASSES = 8
SMAX = 2

TIME_STEP = 0.1
VISCOSITY = 0.5
PENALTY = 4.0
SCREEN = 0.05

AXES = ("gx", "gy")
NODES = 16
NZ = 256
DEPTH = 8
NOISE = 1e-4


def shifted(value, axis, steps):
    count = lax.axis_size(axis)
    pairs = [(source, (source + steps) % count) for source in range(count)]
    return lax.ppermute(value, axis, pairs)


def padded_2(cells, sides, width, closed):
    for axis, dim in sides:
        count = lax.axis_size(axis)
        ends = count if closed else count - 1
        head = lax.slice_in_dim(cells, 0, width, axis=dim)
        tail = lax.slice_in_dim(cells, cells.shape[dim] - width, cells.shape[dim], axis=dim)
        cells = jnp.concatenate(
            [
                lax.ppermute(tail, axis, [(i, (i + 1) % count) for i in range(ends)]),
                cells,
                lax.ppermute(head, axis, [((i + 1) % count, i) for i in range(ends)]),
            ],
            axis=dim,
        )
    return cells


def pad_walls(padded, width):
    row_count = padded.shape[-2]
    inner_rows = row_count - 2 * width
    global_rows = lax.axis_index("gy") * inner_rows + jnp.arange(row_count, dtype=jnp.int32) - width
    total_rows = inner_rows * lax.axis_size("gy")
    inside = ((global_rows >= 0) & (global_rows < total_rows)).astype(padded.dtype)
    return padded * inside[:, None]


def neighbours(padded):
    centre = padded[..., 1:-1, 1:-1, :]
    x_plus = padded[..., 2:, 1:-1, :]
    x_minus = padded[..., :-2, 1:-1, :]
    y_plus = padded[..., 1:-1, 2:, :]
    y_minus = padded[..., 1:-1, :-2, :]
    z_plus = jnp.roll(centre, -1, axis=-1)
    z_minus = jnp.roll(centre, 1, axis=-1)
    return (centre, x_plus, x_minus, y_plus, y_minus, z_plus, z_minus)


def operate(padded):
    centre, x_plus, x_minus, y_plus, y_minus, z_plus, z_minus = neighbours(padded)
    return (6.0 + SCREEN) * centre - (x_plus + x_minus + y_plus + y_minus + z_plus + z_minus)


def advect(padded):
    centre, x_plus, x_minus, y_plus, y_minus, z_plus, z_minus = neighbours(padded)
    laplace = x_plus + x_minus + y_plus + y_minus + z_plus + z_minus - 6.0 * centre
    transport = (
        centre[0:1] * (x_plus - x_minus) * 0.5
        + centre[1:2] * (y_plus - y_minus) * 0.5
        + centre[2:3] * (z_plus - z_minus) * 0.5
    )
    return centre + TIME_STEP * (VISCOSITY * laplace - transport)


def penalize(velocity, cell_swimmer, swimmer_speed):
    target = jnp.zeros_like(velocity)
    for swimmer in range(SWIMMERS):
        target = (
            target
            + (cell_swimmer == swimmer).astype(jnp.float32)[None]
            * swimmer_speed[swimmer][:, None, None, None]
        )
    solid = (cell_swimmer < SWIMMERS).astype(jnp.float32)[None]
    return (velocity + PENALTY * solid * target) / (1.0 + PENALTY * solid)


def divergence(flux_x, flux_y, flux_z):
    return (
        (flux_x[2:] - flux_x[:-2]) * 0.5
        + (flux_y[:, 2:] - flux_y[:, :-2]) * 0.5
        + (jnp.roll(flux_z, -1, axis=2) - jnp.roll(flux_z, 1, axis=2)) * 0.5
    )


def gradient(padded):
    centre, x_plus, x_minus, y_plus, y_minus, z_plus, z_minus = neighbours(padded)
    return jnp.stack([(x_plus - x_minus) * 0.5, (y_plus - y_minus) * 0.5, (z_plus - z_minus) * 0.5])


def plain(velocity, cell_swimmer, swimmer_speed, recentre_cols):
    width_x = velocity.shape[1]

    def search(_, state):
        pressure, residual = state
        extended = pad_walls(padded_2(residual, (("gx", 0), ("gy", 1)), 1, True), 1)
        image = operate(extended)
        norm_sq, curvature = lax.psum((jnp.sum(residual * residual), jnp.sum(residual * image)), AXES)
        alpha = norm_sq / curvature
        return (pressure + alpha * residual, residual - alpha * image)

    def step(step_index, state):
        velocity, _ = state
        offset = recentre_cols[step_index]
        tail_cols = velocity[:, width_x - SMAX :]
        received = shifted(tail_cols, "gx", 1)
        joined = jnp.concatenate([received, velocity], axis=1)
        velocity = lax.dynamic_slice_in_dim(joined, SMAX - offset, width_x, 1)
        padded = pad_walls(padded_2(velocity, (("gx", 1), ("gy", 2)), 1, True), 1)
        velocity = advect(padded)
        velocity = penalize(velocity, cell_swimmer, swimmer_speed)
        flux_x = padded_2(velocity[0], (("gx", 0),), 1, True)
        flux_y = padded_2(velocity[1], (("gy", 1),), 1, False)
        source = -divergence(flux_x, flux_y, velocity[2])
        pressure, _ = lax.fori_loop(0, PASSES, search, (jnp.zeros_like(source), source))
        padded = pad_walls(padded_2(pressure, (("gx", 0), ("gy", 1)), 1, True), 1)
        return (velocity - gradient(padded), pressure)

    start = (velocity, jnp.zeros(velocity.shape[1:], jnp.float32))
    return lax.fori_loop(0, STEPS, step, start)


def tables():
    angle = (np.arange(NODES) + 0.5) * np.pi / NODES
    cheb = np.cos(np.outer(np.arange(NODES), angle))
    moment = np.zeros((NODES, NODES))
    moment[0, 0] = moment[1, 1] = 1.0
    for i in range(1, NODES // 2):
        moment[2 * i, 2 * i], moment[2 * i, 0] = 2.0, -1.0
        moment[2 * i + 1, 2 * i + 1], moment[2 * i + 1, 1] = 2.0, -1.0
    scale = np.full((NODES, 1), 2.0 / NODES)
    scale[0] = 1.0 / NODES
    weight = cheb.T @ (scale * moment)
    weight_map = np.zeros((NODES, 128))
    weight_map[:, :NODES] = weight
    node = (6.0 + SCREEN) - 6.0 * np.cos(angle)
    node = np.broadcast_to(node[:, None], (NODES, NZ // 2))
    coef = np.broadcast_to((scale * cheb)[:PASSES, :, None], (PASSES, NODES, NZ // 2))
    return [np.ascontiguousarray(a, dtype=np.float32) for a in (weight_map, node, coef)]


HALF = NZ // 2


def halves(a):
    return a[:, :HALF], a[:, HALF:]


def z_pair(a, b):
    lane = lax.broadcasted_iota(jnp.int32, a.shape, 1)
    a_next, b_next = pltpu.roll(a, HALF - 1, 1), pltpu.roll(b, HALF - 1, 1)
    a_prev, b_prev = pltpu.roll(a, 1, 1), pltpu.roll(b, 1, 1)
    last, start = lane == HALF - 1, lane == 0
    return (
        (jnp.where(last, b_next, a_next), jnp.where(start, b_prev, a_prev)),
        (jnp.where(last, a_next, b_next), jnp.where(start, a_prev, b_prev)),
    )


def source_kernel(
    info, flags, speed, left, own, right, from_core, from_chip, cell, cell_core, cell_chip, bodied, source, pad, ids, body, *, step
):
    core = info[0]
    joined = 2 - info[1 + step]
    up_flag, down_flag = flags[0], flags[1]

    def put(c, i, value):
        for h, part in enumerate(halves(value)):
            pad[c, i, h, 8:16] = part

    for c in range(3):
        for i in range(4):
            put(c, i, left[c, i])
        for i in range(8):
            put(c, i + 4, own[c, i])
        for i in range(2):
            put(c, i + 12, right[c, i])
        for i in range(14):
            a, b = from_core[c, i], from_chip[c, i]
            up = jnp.where(core == 0, b, a) * up_flag
            down = jnp.where(core == 0, a, b) * down_flag
            for h in range(2):
                pad[c, i, h, 6:8] = halves(up)[h]
                pad[c, i, h, 16:18] = halves(down)[h]
    for i in range(10):
        a, b = cell_core[i], cell_chip[i]
        up, down = jnp.where(core == 0, b, a), jnp.where(core == 0, a, b)
        for h in range(2):
            ids[i, h, 8:16] = halves(cell[i])[h]
            ids[i, h, 6:8] = halves(up)[h]
            ids[i, h, 16:18] = halves(down)[h]

    row = lax.broadcasted_iota(jnp.int32, (8, HALF), 0)
    inside = (jnp.where(row == 0, up_flag, 1.0), jnp.where(row == 0, 1.0, down_flag))

    def move(i, _):
        p = i + 1 + joined
        for block in range(2):
            r = 7 + 8 * block
            centre = [[pad[c, p, h, r : r + 8] for h in range(2)] for c in range(3)]
            beside = [z_pair(*centre[c]) for c in range(3)]
            for h in range(2):
                cells = ids[i, h, r : r + 8]
                marks = [cells == swimmer for swimmer in range(SWIMMERS)]
                factor = jnp.where(cells < SWIMMERS, 1.0 / (1.0 + PENALTY), 1.0) * inside[block]
                for c in range(3):
                    here = centre[c][h]
                    x_plus, x_minus = pad[c, p + 1, h, r : r + 8], pad[c, p - 1, h, r : r + 8]
                    y_plus, y_minus = pad[c, p, h, r + 1 : r + 9], pad[c, p, h, r - 1 : r + 7]
                    z_plus, z_minus = beside[c][h]
                    laplace = x_plus + x_minus + y_plus + y_minus + z_plus + z_minus - 6.0 * here
                    transport = (
                        centre[0][h] * (x_plus - x_minus)
                        + centre[1][h] * (y_plus - y_minus)
                        + centre[2][h] * (z_plus - z_minus)
                    )
                    moved = here + (TIME_STEP * VISCOSITY) * laplace - (TIME_STEP * 0.5) * transport
                    target = jnp.zeros((8, HALF), jnp.float32)
                    for swimmer in range(SWIMMERS):
                        target = jnp.where(marks[swimmer], PENALTY * speed[swimmer, c], target)
                    body[c, i, h, 8 * block : 8 * block + 8] = (moved + target) * factor
        return 0

    for i in range(10):
        move(i, 0)

    for i in range(8):
        b2 = [body[2, i + 1, h, 1:9] for h in range(2)]
        beside = z_pair(*b2)
        for h in range(2):
            lanes = slice(h * HALF, (h + 1) * HALF)
            along_x = body[0, i + 2, h, 1:9] - body[0, i, h, 1:9]
            along_y = body[1, i + 1, h, 2:10] - body[1, i + 1, h, 0:8]
            along_z = beside[h][0] - beside[h][1]
            source[i, :, lanes] = -0.5 * (along_x + along_y + along_z)
            bodied[2, i, :, lanes] = b2[h]
            for c in range(2):
                bodied[c, i, :, lanes] = body[c, i + 1, h, 1:9]


def powers_kernel(info, flags, own, left, right, from_core, from_chip, moments, near, *t):
    core = info[0]
    scale = (flags[0], 1.0, flags[1])

    for i in range(24):
        a, b = from_core[i], from_chip[i]
        up, down = jnp.where(core == 0, b, a) * scale[0], jnp.where(core == 0, a, b) * scale[2]
        middle = (left, own, right)[i // 8][i % 8]
        for h in range(2):
            t[0][i, h, 8:16] = halves(up)[h]
            t[0][i, h, 16:24] = halves(middle)[h]
            t[0][i, h, 24:32] = halves(down)[h]

    for j in range(1, PASSES + 1):
        blocks = (0, 1, 2) if j < PASSES else (1,)

        def level(i, _, j=j, blocks=blocks):
            for block in blocks:
                r = 8 + 8 * block
                factor = scale[block] * (1.0 / 6.0 if j == 1 else 1.0 / 3.0)
                beside = z_pair(t[j - 1][i, 0, r : r + 8], t[j - 1][i, 1, r : r + 8])
                for h in range(2):
                    total = (
                        (t[j - 1][i - 1, h, r : r + 8] + t[j - 1][i + 1, h, r : r + 8])
                        + (t[j - 1][i, h, r - 1 : r + 7] + t[j - 1][i, h, r + 1 : r + 9])
                        + (beside[h][0] + beside[h][1])
                    )
                    value = total * factor
                    if j > 1:
                        value = value - t[j - 2][i, h, r : r + 8]
                    t[j][i, h, r : r + 8] = value
            return 0

        for i in range(j, 24 - j):
            level(i, 0)

    def product(i, sums):
        out = list(sums)
        for h in range(2):
            values = [t[j][i, h, 16:24] for j in range(PASSES + 1)]
            for j in range(PASSES):
                out[2 * j] = out[2 * j] + values[j] * values[j]
                out[2 * j + 1] = out[2 * j + 1] + values[j] * values[j + 1]
        return tuple(out)

    zero = jnp.zeros((8, HALF), jnp.float32)
    sums = (zero,) * NODES
    for i in range(DEPTH, 2 * DEPTH):
        sums = product(i, sums)
    lines = [jnp.sum(a, axis=0, keepdims=True) for a in sums]
    block = jnp.concatenate(lines + [jnp.zeros((128 - NODES, 128), jnp.float32)], axis=0)
    line = jnp.sum(block.T, axis=0, keepdims=True)
    moments[...] = jnp.broadcast_to(line, moments.shape)

    def keep(i, _):
        for j in range(PASSES):
            for h in range(2):
                near[j, i, h, 0:8] = t[j][i + DEPTH - 1, h, 15:23]
                near[j, i, h, 8:16] = t[j][i + DEPTH - 1, h, 23:31]
        return 0

    for i in range(10):
        keep(i, 0)


def lengths(moments, weight_map, node, coef):
    line = jnp.sum(moments[...], axis=0, keepdims=True)
    weight = jnp.sum(weight_map[...] * line, axis=1, keepdims=True)
    weight = jnp.broadcast_to(weight, (NODES, HALF))
    first = jnp.sum(weight, axis=0, keepdims=True)
    value = node[...]
    residual = jnp.ones((NODES, HALF), jnp.float32)
    search = jnp.zeros((NODES, HALF), jnp.float32)
    good = jnp.ones((1, HALF), jnp.float32)
    for _ in range(PASSES):
        square = residual * residual
        norm_sq = jnp.sum(weight * square, axis=0, keepdims=True)
        curvature = jnp.sum(weight * square * value, axis=0, keepdims=True)
        noise = NOISE * first * jnp.sum(square, axis=0, keepdims=True)
        noise_image = NOISE * first * jnp.sum(square * value, axis=0, keepdims=True)
        good = jnp.where((norm_sq > noise) & (curvature > noise_image), good, 0.0)
        alpha = norm_sq / curvature
        search = search + alpha * residual
        residual = residual - alpha * value * residual
    terms = [jnp.sum(coef[j] * search, axis=0, keepdims=True) for j in range(PASSES)]
    return terms, good


def correct(terms, near, bodied, emit, p):
    def combine(i, _):
        for h in range(2):
            for r in (0, 8):
                total = terms[0] * near[0, i, h, r : r + 8]
                for j in range(1, PASSES):
                    total = total + terms[j] * near[j, i, h, r : r + 8]
                p[i, h, r : r + 8] = total
        return 0

    for i in range(10):
        combine(i, 0)
    for i in range(8):
        own = [p[i + 1, h, 1:9] for h in range(2)]
        beside = z_pair(*own)
        for h in range(2):
            lanes = slice(h * HALF, (h + 1) * HALF)
            emit(0, i, lanes, bodied[0, i, :, lanes] - 0.5 * (p[i + 2, h, 1:9] - p[i, h, 1:9]))
            emit(1, i, lanes, bodied[1, i, :, lanes] - 0.5 * (p[i + 1, h, 2:10] - p[i + 1, h, 0:8]))
            emit(2, i, lanes, bodied[2, i, :, lanes] - 0.5 * (beside[h][0] - beside[h][1]))
            emit(3, i, lanes, own[h])


def inner_step_kernel(moments, weight_map, node, coef, near, bodied, good_out, velocity, p):
    terms, good = lengths(moments, weight_map, node, coef)
    good_out[...] = good

    def emit(c, i, lanes, value):
        if c < 3:
            velocity[c, i, :, lanes] = value

    correct(terms, near, bodied, emit, p)


def last_step_kernel(info, moments, weight_map, node, coef, near, bodied, good_in, good_out, kept, sent, p, fields):
    terms, good = lengths(moments, weight_map, node, coef)
    good_out[0] = (jnp.min(good * good_in[...]) > 0.5).astype(jnp.int32)
    core = info[0]

    def emit(c, i, lanes, value):
        fields[c, i, :, lanes] = value

    correct(terms, near, bodied, emit, p)
    for i in range(4):
        for c in range(4):
            kept[c, i] = fields[c, 4 * core + i]
            sent[c, i] = fields[c, 4 * (1 - core) + i]


SMEM = pl.BlockSpec(memory_space=pltpu.SMEM)
VMEM = pl.BlockSpec(memory_space=pltpu.VMEM)


def call(kernel, args, smem, outs, scratch, flags_out=0):
    specs, shapes = [VMEM] * len(outs), [jax.ShapeDtypeStruct(o, jnp.float32) for o in outs]
    if flags_out:
        specs, shapes = [SMEM] + specs, [jax.ShapeDtypeStruct((1,), jnp.int32)] + shapes
    return pl.pallas_call(
        kernel,
        in_specs=[SMEM] * smem + [VMEM] * (len(args) - smem),
        out_specs=specs,
        out_shape=shapes,
        scratch_shapes=[pltpu.VMEM(o, jnp.float32) for o in scratch],
        compiler_params=pltpu.CompilerParams(vmem_limit_bytes=24 * 1024 * 1024),
        cost_estimate=pl.CostEstimate(flops=1_000_000, bytes_accessed=1_000_000, transcendentals=0),
    )(*args)


def routes(count_x, count_y):
    chips = count_x // 2

    def pairs(target):
        out = []
        for chip in range(chips):
            for core in range(2):
                for y in range(count_y):
                    to = target(chip, core, y)
                    source = (2 * chip + core) * count_y + y
                    out.append((source, (2 * (to[0] % chips) + to[1]) * count_y + to[2]))
        return out

    def across(chip, core, y):
        return (chip, 1 - core, (y + (1 if core else -1)) % count_y)

    return {
        "core": pairs(lambda chip, core, y: (chip, 1 - core, y)),
        "facing": pairs(lambda chip, core, y: (chip + (1 if core else -1), 1 - core, y)),
        "right": pairs(lambda chip, core, y: (chip + 1, core, y)),
        "left": pairs(lambda chip, core, y: (chip - 1, core, y)),
        "across": pairs(across),
    }


def body(velocity, cell_swimmer, swimmer_speed, recentre_cols, *, count_x, count_y):
    route = routes(count_x, count_y)
    send = lambda value, name: lax.ppermute(value, AXES, route[name])
    core = lax.axis_index("gx") % 2
    y = lax.axis_index("gy")
    flags = jnp.stack([(y > 0) | (core == 1), (y < count_y - 1) | (core == 0)]).astype(jnp.float32)
    info = jnp.stack([core, recentre_cols[0], recentre_cols[1]]).astype(jnp.int32)
    weight_map, node, coef = (jnp.asarray(a) for a in tables())
    first = core == 0
    pick = lambda a, b: jnp.where(first, a, b)

    cells = cell_swimmer.astype(jnp.float32)
    rows = velocity.reshape(12, 16, NZ)
    outer = send(jnp.concatenate([rows, pick(cells[0:1], cells[3:4])], axis=0), "facing")
    chunk = jnp.concatenate([rows, cells], axis=0)
    theirs = send(pick(chunk[:, 8:16], chunk[:, 0:8]), "core")
    mine = pick(chunk[:, 0:8], chunk[:, 8:16])
    outer_theirs = send(pick(outer[:, 8:16], outer[:, 0:8]), "core")
    outer_mine = pick(outer[:, 0:8], outer[:, 8:16])
    low, high = pick(mine, theirs), pick(theirs, mine)
    outer_low, outer_high = pick(outer_mine, outer_theirs), pick(outer_theirs, outer_mine)
    planes = lambda a: a[0:12].reshape(3, 4, 8, NZ)
    own = jnp.concatenate([planes(low), planes(high)], axis=1)
    left, right = planes(outer_low), planes(outer_high)[:, 0:2]
    cell = jnp.concatenate([outer_low[12:13], low[12:16], high[12:16], outer_high[12:13]], axis=0)

    for step in range(STEPS):
        if step:
            left = send(own[:, 4:8], "right")
            right = send(own[:, 0:2], "left")
        joined = jnp.concatenate([left, own, right], axis=1)
        if not step:
            spare = jnp.concatenate([cell, cell[0:4]], axis=0)
            joined = jnp.concatenate([joined, spare[None]], axis=0)
        top, bottom = joined[:, :, 0:2], joined[:, :, 6:8]
        from_core, from_chip = send(pick(bottom, top), "core"), send(pick(top, bottom), "across")
        if not step:
            cell_core, cell_chip = from_core[3, 0:10], from_chip[3, 0:10]
        bodied, source = call(
            functools.partial(source_kernel, step=step),
            (info, flags, swimmer_speed, left, own, right, from_core, from_chip, cell, cell_core, cell_chip),
            3,
            [(3, 8, 8, NZ), (8, 8, NZ)],
            [(3, 14, 2, 24, HALF), (10, 2, 24, HALF), (3, 10, 2, 16, HALF)],
        )
        s_left = send(source, "right")
        s_right = send(source, "left")
        column = jnp.concatenate([s_left, source, s_right], axis=0)
        moments, near = call(
            powers_kernel,
            (info, flags, source, s_left, s_right, send(column, "core"), send(column, "across")),
            2,
            [(count_x * count_y, 128), (PASSES, 10, 2, 16, HALF)],
            [(24, 2, 40, HALF)] * (PASSES + 1),
        )
        moments = lax.all_to_all(moments, AXES, 0, 0)
        shared = (moments, weight_map, node, coef, near, bodied)
        if step < STEPS - 1:
            good, own = call(inner_step_kernel, shared, 0, [(1, HALF), (3, 8, 8, NZ)], [(10, 2, 16, HALF)])
        else:
            good, kept, sent = call(
                last_step_kernel,
                (info,) + shared + (good,),
                1,
                [(4, 4, 8, NZ), (4, 4, 8, NZ)],
                [(10, 2, 16, HALF), (4, 8, 8, NZ)],
                flags_out=1,
            )

    def finish(_):
        got = send(sent, "core")
        fields = jnp.concatenate([pick(kept, got), pick(got, kept)], axis=2)
        return (fields[0:3], fields[3])

    def again(_):
        return plain(velocity, cell_swimmer, swimmer_speed, recentre_cols)

    return lax.cond(good[0] > 0, finish, again, None)


def solution(mesh):
    placed = (P(None, "gx", "gy", None), P("gx", "gy", None), P(), P())
    return jax.shard_map(
        functools.partial(body, count_x=mesh.shape["gx"], count_y=mesh.shape["gy"]),
        mesh=mesh,
        in_specs=placed,
        out_specs=(P(None, "gx", "gy", None), P("gx", "gy", None)),
        check_vma=False,
    )
```

```python
import functools

import jax
import jax.numpy as jnp
import numpy as np
from jax import lax
from jax.experimental import pallas as pl
from jax.experimental.pallas import tpu as pltpu
from jax.sharding import PartitionSpec as P

SWIMMERS = 8
STEPS = 2
PASSES = 8
SMAX = 2

TIME_STEP = 0.1
VISCOSITY = 0.5
PENALTY = 4.0
SCREEN = 0.05

AXES = ("gx", "gy")
NODES = 16
NZ = 256
DEPTH = 8
NOISE = 1e-4


def shifted(value, axis, steps):
    count = lax.axis_size(axis)
    pairs = [(source, (source + steps) % count) for source in range(count)]
    return lax.ppermute(value, axis, pairs)


def padded_2(cells, sides, width, closed):
    for axis, dim in sides:
        count = lax.axis_size(axis)
        ends = count if closed else count - 1
        head = lax.slice_in_dim(cells, 0, width, axis=dim)
        tail = lax.slice_in_dim(cells, cells.shape[dim] - width, cells.shape[dim], axis=dim)
        cells = jnp.concatenate(
            [
                lax.ppermute(tail, axis, [(i, (i + 1) % count) for i in range(ends)]),
                cells,
                lax.ppermute(head, axis, [((i + 1) % count, i) for i in range(ends)]),
            ],
            axis=dim,
        )
    return cells


def pad_walls(padded, width):
    row_count = padded.shape[-2]
    inner_rows = row_count - 2 * width
    global_rows = lax.axis_index("gy") * inner_rows + jnp.arange(row_count, dtype=jnp.int32) - width
    total_rows = inner_rows * lax.axis_size("gy")
    inside = ((global_rows >= 0) & (global_rows < total_rows)).astype(padded.dtype)
    return padded * inside[:, None]


def neighbours(padded):
    centre = padded[..., 1:-1, 1:-1, :]
    x_plus = padded[..., 2:, 1:-1, :]
    x_minus = padded[..., :-2, 1:-1, :]
    y_plus = padded[..., 1:-1, 2:, :]
    y_minus = padded[..., 1:-1, :-2, :]
    z_plus = jnp.roll(centre, -1, axis=-1)
    z_minus = jnp.roll(centre, 1, axis=-1)
    return (centre, x_plus, x_minus, y_plus, y_minus, z_plus, z_minus)


def operate(padded):
    centre, x_plus, x_minus, y_plus, y_minus, z_plus, z_minus = neighbours(padded)
    return (6.0 + SCREEN) * centre - (x_plus + x_minus + y_plus + y_minus + z_plus + z_minus)


def advect(padded):
    centre, x_plus, x_minus, y_plus, y_minus, z_plus, z_minus = neighbours(padded)
    laplace = x_plus + x_minus + y_plus + y_minus + z_plus + z_minus - 6.0 * centre
    transport = (
        centre[0:1] * (x_plus - x_minus) * 0.5
        + centre[1:2] * (y_plus - y_minus) * 0.5
        + centre[2:3] * (z_plus - z_minus) * 0.5
    )
    return centre + TIME_STEP * (VISCOSITY * laplace - transport)


def penalize(velocity, cell_swimmer, swimmer_speed):
    target = jnp.zeros_like(velocity)
    for swimmer in range(SWIMMERS):
        target = (
            target
            + (cell_swimmer == swimmer).astype(jnp.float32)[None]
            * swimmer_speed[swimmer][:, None, None, None]
        )
    solid = (cell_swimmer < SWIMMERS).astype(jnp.float32)[None]
    return (velocity + PENALTY * solid * target) / (1.0 + PENALTY * solid)


def divergence(flux_x, flux_y, flux_z):
    return (
        (flux_x[2:] - flux_x[:-2]) * 0.5
        + (flux_y[:, 2:] - flux_y[:, :-2]) * 0.5
        + (jnp.roll(flux_z, -1, axis=2) - jnp.roll(flux_z, 1, axis=2)) * 0.5
    )


def gradient(padded):
    centre, x_plus, x_minus, y_plus, y_minus, z_plus, z_minus = neighbours(padded)
    return jnp.stack([(x_plus - x_minus) * 0.5, (y_plus - y_minus) * 0.5, (z_plus - z_minus) * 0.5])


def plain(velocity, cell_swimmer, swimmer_speed, recentre_cols):
    width_x = velocity.shape[1]

    def search(_, state):
        pressure, residual = state
        extended = pad_walls(padded_2(residual, (("gx", 0), ("gy", 1)), 1, True), 1)
        image = operate(extended)
        norm_sq, curvature = lax.psum((jnp.sum(residual * residual), jnp.sum(residual * image)), AXES)
        alpha = norm_sq / curvature
        return (pressure + alpha * residual, residual - alpha * image)

    def step(step_index, state):
        velocity, _ = state
        offset = recentre_cols[step_index]
        tail_cols = velocity[:, width_x - SMAX :]
        received = shifted(tail_cols, "gx", 1)
        joined = jnp.concatenate([received, velocity], axis=1)
        velocity = lax.dynamic_slice_in_dim(joined, SMAX - offset, width_x, 1)
        padded = pad_walls(padded_2(velocity, (("gx", 1), ("gy", 2)), 1, True), 1)
        velocity = advect(padded)
        velocity = penalize(velocity, cell_swimmer, swimmer_speed)
        flux_x = padded_2(velocity[0], (("gx", 0),), 1, True)
        flux_y = padded_2(velocity[1], (("gy", 1),), 1, False)
        source = -divergence(flux_x, flux_y, velocity[2])
        pressure, _ = lax.fori_loop(0, PASSES, search, (jnp.zeros_like(source), source))
        padded = pad_walls(padded_2(pressure, (("gx", 0), ("gy", 1)), 1, True), 1)
        return (velocity - gradient(padded), pressure)

    start = (velocity, jnp.zeros(velocity.shape[1:], jnp.float32))
    return lax.fori_loop(0, STEPS, step, start)


def tables():
    angle = (np.arange(NODES) + 0.5) * np.pi / NODES
    cheb = np.cos(np.outer(np.arange(NODES), angle))
    moment = np.zeros((NODES, NODES))
    moment[0, 0] = moment[1, 1] = 1.0
    for i in range(1, NODES // 2):
        moment[2 * i, 2 * i], moment[2 * i, 0] = 2.0, -1.0
        moment[2 * i + 1, 2 * i + 1], moment[2 * i + 1, 1] = 2.0, -1.0
    scale = np.full((NODES, 1), 2.0 / NODES)
    scale[0] = 1.0 / NODES
    weight = cheb.T @ (scale * moment)
    weight_map = np.zeros((NODES, 128))
    weight_map[:, :NODES] = weight
    node = (6.0 + SCREEN) - 6.0 * np.cos(angle)
    node = np.broadcast_to(node[:, None], (NODES, NZ // 2))
    coef = np.broadcast_to((scale * cheb)[:PASSES, :, None], (PASSES, NODES, NZ // 2))
    return [np.ascontiguousarray(a, dtype=np.float32) for a in (weight_map, node, coef)]


HALF = NZ // 2


def halves(a):
    return a[:, :HALF], a[:, HALF:]


def z_pair(a, b):
    lane = lax.broadcasted_iota(jnp.int32, a.shape, 1)
    a_next, b_next = pltpu.roll(a, HALF - 1, 1), pltpu.roll(b, HALF - 1, 1)
    a_prev, b_prev = pltpu.roll(a, 1, 1), pltpu.roll(b, 1, 1)
    last, start = lane == HALF - 1, lane == 0
    return (
        (jnp.where(last, b_next, a_next), jnp.where(start, b_prev, a_prev)),
        (jnp.where(last, a_next, b_next), jnp.where(start, a_prev, b_prev)),
    )


def source_kernel(
    info, flags, speed, left, own, right, from_core, from_chip, cell, cell_core, cell_chip, bodied, source, pad, ids, body, *, step
):
    core = info[0]
    joined = 2 - info[1 + step]
    up_flag, down_flag = flags[0], flags[1]

    def put(c, i, value):
        for h, part in enumerate(halves(value)):
            pad[c, i, h, 8:16] = part

    for c in range(3):
        for i in range(4):
            put(c, i, left[c, i])
        for i in range(8):
            put(c, i + 4, own[c, i])
        for i in range(2):
            put(c, i + 12, right[c, i])
        for i in range(1, 13):
            a, b = from_core[c, i - 1], from_chip[c, i - 1]
            up = jnp.where(core == 0, b, a) * up_flag
            down = jnp.where(core == 0, a, b) * down_flag
            for h in range(2):
                pad[c, i, h, 6:8] = halves(up)[h]
                pad[c, i, h, 16:18] = halves(down)[h]
    for i in range(10):
        a, b = cell_core[i], cell_chip[i]
        up, down = jnp.where(core == 0, b, a), jnp.where(core == 0, a, b)
        for h in range(2):
            ids[i, h, 8:16] = halves(cell[i])[h]
            ids[i, h, 6:8] = halves(up)[h]
            ids[i, h, 16:18] = halves(down)[h]

    row = lax.broadcasted_iota(jnp.int32, (8, HALF), 0)
    inside = (jnp.where(row == 0, up_flag, 1.0), jnp.where(row == 0, 1.0, down_flag))

    def move(i, _):
        p = i + 1 + joined
        for block in range(2):
            r = 7 + 8 * block
            centre = [[pad[c, p, h, r : r + 8] for h in range(2)] for c in range(3)]
            beside = [z_pair(*centre[c]) for c in range(3)]
            for h in range(2):
                cells = ids[i, h, r : r + 8]
                marks = [cells == swimmer for swimmer in range(SWIMMERS)]
                factor = jnp.where(cells < SWIMMERS, 1.0 / (1.0 + PENALTY), 1.0) * inside[block]
                for c in range(3):
                    here = centre[c][h]
                    x_plus, x_minus = pad[c, p + 1, h, r : r + 8], pad[c, p - 1, h, r : r + 8]
                    y_plus, y_minus = pad[c, p, h, r + 1 : r + 9], pad[c, p, h, r - 1 : r + 7]
                    z_plus, z_minus = beside[c][h]
                    laplace = x_plus + x_minus + y_plus + y_minus + z_plus + z_minus - 6.0 * here
                    transport = (
                        centre[0][h] * (x_plus - x_minus)
                        + centre[1][h] * (y_plus - y_minus)
                        + centre[2][h] * (z_plus - z_minus)
                    )
                    moved = here + (TIME_STEP * VISCOSITY) * laplace - (TIME_STEP * 0.5) * transport
                    target = jnp.zeros((8, HALF), jnp.float32)
                    for swimmer in range(SWIMMERS):
                        target = jnp.where(marks[swimmer], PENALTY * speed[swimmer, c], target)
                    body[c, i, h, 8 * block : 8 * block + 8] = (moved + target) * factor
        return 0

    for i in range(10):
        move(i, 0)

    for i in range(8):
        b2 = [body[2, i + 1, h, 1:9] for h in range(2)]
        beside = z_pair(*b2)
        for h in range(2):
            lanes = slice(h * HALF, (h + 1) * HALF)
            along_x = body[0, i + 2, h, 1:9] - body[0, i, h, 1:9]
            along_y = body[1, i + 1, h, 2:10] - body[1, i + 1, h, 0:8]
            along_z = beside[h][0] - beside[h][1]
            source[i, :, lanes] = -0.5 * (along_x + along_y + along_z)
            bodied[2, i, :, lanes] = b2[h]
            for c in range(2):
                bodied[c, i, :, lanes] = body[c, i + 1, h, 1:9]


def powers_kernel(info, flags, own, left, right, from_core, from_chip, moments, near, *t):
    core = info[0]
    scale = (flags[0], 1.0, flags[1])

    for i in range(24):
        k = min(max(i - 1, 0), 21)
        a, b = from_core[k], from_chip[k]
        up, down = jnp.where(core == 0, b, a) * scale[0], jnp.where(core == 0, a, b) * scale[2]
        middle = (left, own, right)[i // 8][i % 8]
        for h in range(2):
            t[0][i, h, 8:16] = halves(up)[h]
            t[0][i, h, 16:24] = halves(middle)[h]
            t[0][i, h, 24:32] = halves(down)[h]

    for j in range(1, PASSES + 1):
        blocks = (0, 1, 2) if j < PASSES else (1,)

        def level(i, _, j=j, blocks=blocks):
            for block in blocks:
                r = 8 + 8 * block
                factor = scale[block] * (1.0 / 6.0 if j == 1 else 1.0 / 3.0)
                beside = z_pair(t[j - 1][i, 0, r : r + 8], t[j - 1][i, 1, r : r + 8])
                for h in range(2):
                    total = (
                        (t[j - 1][i - 1, h, r : r + 8] + t[j - 1][i + 1, h, r : r + 8])
                        + (t[j - 1][i, h, r - 1 : r + 7] + t[j - 1][i, h, r + 1 : r + 9])
                        + (beside[h][0] + beside[h][1])
                    )
                    value = total * factor
                    if j > 1:
                        value = value - t[j - 2][i, h, r : r + 8]
                    t[j][i, h, r : r + 8] = value
            return 0

        for i in range(j, 24 - j):
            level(i, 0)

    def product(i, sums):
        out = list(sums)
        for h in range(2):
            values = [t[j][i, h, 16:24] for j in range(PASSES + 1)]
            for j in range(PASSES):
                out[2 * j] = out[2 * j] + values[j] * values[j]
                out[2 * j + 1] = out[2 * j + 1] + values[j] * values[j + 1]
        return tuple(out)

    zero = jnp.zeros((8, HALF), jnp.float32)
    sums = (zero,) * NODES
    for i in range(DEPTH, 2 * DEPTH):
        sums = product(i, sums)
    lines = [jnp.sum(a, axis=0, keepdims=True) for a in sums]
    block = jnp.concatenate(lines + [jnp.zeros((128 - NODES, 128), jnp.float32)], axis=0)
    line = jnp.sum(block.T, axis=0, keepdims=True)
    moments[...] = jnp.broadcast_to(line, moments.shape)

    def keep(i, _):
        for j in range(PASSES):
            for h in range(2):
                near[j, i, h, 0:8] = t[j][i + DEPTH - 1, h, 15:23]
                near[j, i, h, 8:16] = t[j][i + DEPTH - 1, h, 23:31]
        return 0

    for i in range(10):
        keep(i, 0)


def lengths(moments, weight_map, node, coef):
    line = jnp.sum(moments[...], axis=0, keepdims=True)
    weight = jnp.sum(weight_map[...] * line, axis=1, keepdims=True)
    weight = jnp.broadcast_to(weight, (NODES, HALF))
    first = jnp.sum(weight, axis=0, keepdims=True)
    value = node[...]
    residual = jnp.ones((NODES, HALF), jnp.float32)
    search = jnp.zeros((NODES, HALF), jnp.float32)
    good = jnp.ones((1, HALF), jnp.float32)
    for _ in range(PASSES):
        square = residual * residual
        norm_sq = jnp.sum(weight * square, axis=0, keepdims=True)
        curvature = jnp.sum(weight * square * value, axis=0, keepdims=True)
        noise = NOISE * first * jnp.sum(square, axis=0, keepdims=True)
        noise_image = NOISE * first * jnp.sum(square * value, axis=0, keepdims=True)
        good = jnp.where((norm_sq > noise) & (curvature > noise_image), good, 0.0)
        alpha = norm_sq / curvature
        search = search + alpha * residual
        residual = residual - alpha * value * residual
    terms = [jnp.sum(coef[j] * search, axis=0, keepdims=True) for j in range(PASSES)]
    return terms, good


def combine(terms, near, p):
    for i in range(10):
        for h in range(2):
            for r in (0, 8):
                total = terms[0] * near[0, i, h, r : r + 8]
                for j in range(1, PASSES):
                    total = total + terms[j] * near[j, i, h, r : r + 8]
                p[i, h, r : r + 8] = total


def corrected(i, bodied, p, put):
    own = [p[i + 1, h, 1:9] for h in range(2)]
    beside = z_pair(*own)
    for h in range(2):
        lanes = slice(h * HALF, (h + 1) * HALF)
        put(0, lanes, bodied[0, i, :, lanes] - 0.5 * (p[i + 2, h, 1:9] - p[i, h, 1:9]))
        put(1, lanes, bodied[1, i, :, lanes] - 0.5 * (p[i + 1, h, 2:10] - p[i + 1, h, 0:8]))
        put(2, lanes, bodied[2, i, :, lanes] - 0.5 * (beside[h][0] - beside[h][1]))
        put(3, lanes, own[h])


def inner_step_kernel(moments, weight_map, node, coef, near, bodied, good_out, velocity, p):
    terms, good = lengths(moments, weight_map, node, coef)
    good_out[...] = good
    combine(terms, near, p)
    for i in range(8):

        def put(c, lanes, value, i=i):
            if c < 3:
                velocity[c, i, :, lanes] = value

        corrected(i, bodied, p, put)


def last_step_kernel(info, moments, weight_map, node, coef, near, bodied, good_in, good_out, kept, sent, p):
    terms, good = lengths(moments, weight_map, node, coef)
    good_out[0] = (jnp.min(good * good_in[...]) > 0.5).astype(jnp.int32)
    core = info[0]
    combine(terms, near, p)
    for i in range(4):
        for out, start in ((sent, 4 * (1 - core)), (kept, 4 * core)):

            def put(c, lanes, value, i=i, out=out):
                out[c, i, :, lanes] = value

            corrected(start + i, bodied, p, put)


def place_kernel(info, kept, got, velocity, pressure):
    first = info[0] == 0
    for i in range(4):
        for c in range(4):
            a, b = kept[c, i], got[c, i]
            low, high = jnp.where(first, a, b), jnp.where(first, b, a)
            if c < 3:
                velocity[c, i, 0:8] = low
                velocity[c, i, 8:16] = high
            else:
                pressure[i, 0:8] = low
                pressure[i, 8:16] = high


SMEM = pl.BlockSpec(memory_space=pltpu.SMEM)
VMEM = pl.BlockSpec(memory_space=pltpu.VMEM)


def call(kernel, args, smem, outs, scratch, flags_out=0):
    specs, shapes = [VMEM] * len(outs), [jax.ShapeDtypeStruct(o, jnp.float32) for o in outs]
    if flags_out:
        specs, shapes = [SMEM] + specs, [jax.ShapeDtypeStruct((1,), jnp.int32)] + shapes
    return pl.pallas_call(
        kernel,
        in_specs=[SMEM] * smem + [VMEM] * (len(args) - smem),
        out_specs=specs,
        out_shape=shapes,
        scratch_shapes=[pltpu.VMEM(o, jnp.float32) for o in scratch],
        compiler_params=pltpu.CompilerParams(vmem_limit_bytes=24 * 1024 * 1024),
        cost_estimate=pl.CostEstimate(flops=1_000_000, bytes_accessed=1_000_000, transcendentals=0),
    )(*args)


def routes(count_x, count_y):
    chips = count_x // 2

    def pairs(target):
        out = []
        for chip in range(chips):
            for core in range(2):
                for y in range(count_y):
                    to = target(chip, core, y)
                    source = (2 * chip + core) * count_y + y
                    out.append((source, (2 * (to[0] % chips) + to[1]) * count_y + to[2]))
        return out

    def across(chip, core, y):
        return (chip, 1 - core, (y + (1 if core else -1)) % count_y)

    return {
        "core": pairs(lambda chip, core, y: (chip, 1 - core, y)),
        "facing": pairs(lambda chip, core, y: (chip + (1 if core else -1), 1 - core, y)),
        "inner": pairs(lambda chip, core, y: (chip + (1 if chip % 2 == 0 else -1), core, y)),
        "outer": pairs(lambda chip, core, y: (chip + (-1 if chip % 2 == 0 else 1), core, y)),
        "across": pairs(across),
    }


def body(velocity, cell_swimmer, swimmer_speed, recentre_cols, *, count_x, count_y):
    route = routes(count_x, count_y)
    send = lambda value, name: lax.ppermute(value, AXES, route[name])
    core = lax.axis_index("gx") % 2
    y = lax.axis_index("gy")
    flags = jnp.stack([(y > 0) | (core == 1), (y < count_y - 1) | (core == 0)]).astype(jnp.float32)
    info = jnp.stack([core, recentre_cols[0], recentre_cols[1]]).astype(jnp.int32)
    weight_map, node, coef = (jnp.asarray(a) for a in tables())
    first = core == 0
    pick = lambda a, b: jnp.where(first, a, b)
    even = (lax.axis_index("gx") // 2) % 2 == 0

    def beside(to_left, to_right):
        outer = send(jnp.where(even, to_left, to_right), "outer")
        inner = send(jnp.where(even, to_right, to_left), "inner")
        return jnp.where(even, outer, inner), jnp.where(even, inner, outer)


    cells = cell_swimmer.astype(jnp.float32)
    rows = velocity.reshape(12, 16, NZ)
    outer = send(jnp.concatenate([rows, pick(cells[0:1], cells[3:4])], axis=0), "facing")
    chunk = jnp.concatenate([rows, cells], axis=0)
    theirs = send(pick(chunk[:, 8:16], chunk[:, 0:8]), "core")
    mine = pick(chunk[:, 0:8], chunk[:, 8:16])
    outer_theirs = send(pick(outer[:, 8:16], outer[:, 0:8]), "core")
    outer_mine = pick(outer[:, 0:8], outer[:, 8:16])
    low, high = pick(mine, theirs), pick(theirs, mine)
    outer_low, outer_high = pick(outer_mine, outer_theirs), pick(outer_theirs, outer_mine)
    planes = lambda a: a[0:12].reshape(3, 4, 8, NZ)
    own = jnp.concatenate([planes(low), planes(high)], axis=1)
    left, right = planes(outer_low), planes(outer_high)[:, 0:2]
    cell = jnp.concatenate([outer_low[12:13], low[12:16], high[12:16], outer_high[12:13]], axis=0)

    for step in range(STEPS):
        if step:
            left, right = beside(own[:, 0:4], own[:, 4:8])
            right = right[:, 0:2]
        joined = jnp.concatenate([left, own, right], axis=1)
        if not step:
            spare = jnp.concatenate([cell[0:1], cell, cell[0:3]], axis=0)
            joined = jnp.concatenate([joined, spare[None]], axis=0)
        top, bottom = joined[:, 1:13, 0:2], joined[:, 1:13, 6:8]
        from_core, from_chip = send(pick(bottom, top), "core"), send(pick(top, bottom), "across")
        if not step:
            cell_core, cell_chip = from_core[3, 0:10], from_chip[3, 0:10]
        bodied, source = call(
            functools.partial(source_kernel, step=step),
            (info, flags, swimmer_speed, left, own, right, from_core, from_chip, cell, cell_core, cell_chip),
            3,
            [(3, 8, 8, NZ), (8, 8, NZ)],
            [(3, 14, 2, 24, HALF), (10, 2, 24, HALF), (3, 10, 2, 16, HALF)],
        )
        s_left, s_right = beside(source, source)
        column = jnp.concatenate([s_left[1:], source, s_right[:7]], axis=0)
        moments, near = call(
            powers_kernel,
            (info, flags, source, s_left, s_right, send(column, "core"), send(column, "across")),
            2,
            [(count_x * count_y, 128), (PASSES, 10, 2, 16, HALF)],
            [(24, 2, 40, HALF)] * (PASSES + 1),
        )
        moments = lax.all_to_all(moments, AXES, 0, 0)
        shared = (moments, weight_map, node, coef, near, bodied)
        if step < STEPS - 1:
            good, own = call(inner_step_kernel, shared, 0, [(1, HALF), (3, 8, 8, NZ)], [(10, 2, 16, HALF)])
        else:
            good, kept, sent = call(
                last_step_kernel,
                (info,) + shared + (good,),
                1,
                [(4, 4, 8, NZ), (4, 4, 8, NZ)],
                [(10, 2, 16, HALF)],
                flags_out=1,
            )

    def finish(_):
        got = send(sent, "core")
        return tuple(call(place_kernel, (info, kept, got), 1, [(3, 4, 16, NZ), (4, 16, NZ)], []))

    def again(_):
        return plain(velocity, cell_swimmer, swimmer_speed, recentre_cols)

    return lax.cond(good[0] > 0, finish, again, None)


def solution(mesh):
    placed = (P(None, "gx", "gy", None), P("gx", "gy", None), P(), P())
    return jax.shard_map(
        functools.partial(body, count_x=mesh.shape["gx"], count_y=mesh.shape["gy"]),
        mesh=mesh,
        in_specs=placed,
        out_specs=(P(None, "gx", "gy", None), P("gx", "gy", None)),
        check_vma=False,
    )
```

```python
import functools

import jax
import jax.numpy as jnp
import numpy as np
from jax import lax
from jax.experimental import pallas as pl
from jax.experimental.pallas import tpu as pltpu
from jax.sharding import PartitionSpec as P

SWIMMERS = 8
STEPS = 2
PASSES = 8
SMAX = 2

TIME_STEP = 0.1
VISCOSITY = 0.5
PENALTY = 4.0
SCREEN = 0.05

AXES = ("gx", "gy")
NODES = 16
NZ = 256
DEPTH = 8
NOISE = 1e-5


def shifted(value, axis, steps):
    count = lax.axis_size(axis)
    pairs = [(source, (source + steps) % count) for source in range(count)]
    return lax.ppermute(value, axis, pairs)


def padded_2(cells, sides, width, closed):
    for axis, dim in sides:
        count = lax.axis_size(axis)
        ends = count if closed else count - 1
        head = lax.slice_in_dim(cells, 0, width, axis=dim)
        tail = lax.slice_in_dim(cells, cells.shape[dim] - width, cells.shape[dim], axis=dim)
        cells = jnp.concatenate(
            [
                lax.ppermute(tail, axis, [(i, (i + 1) % count) for i in range(ends)]),
                cells,
                lax.ppermute(head, axis, [((i + 1) % count, i) for i in range(ends)]),
            ],
            axis=dim,
        )
    return cells


def pad_walls(padded, width):
    row_count = padded.shape[-2]
    inner_rows = row_count - 2 * width
    global_rows = lax.axis_index("gy") * inner_rows + jnp.arange(row_count, dtype=jnp.int32) - width
    total_rows = inner_rows * lax.axis_size("gy")
    inside = ((global_rows >= 0) & (global_rows < total_rows)).astype(padded.dtype)
    return padded * inside[:, None]


def neighbours(padded):
    centre = padded[..., 1:-1, 1:-1, :]
    x_plus = padded[..., 2:, 1:-1, :]
    x_minus = padded[..., :-2, 1:-1, :]
    y_plus = padded[..., 1:-1, 2:, :]
    y_minus = padded[..., 1:-1, :-2, :]
    z_plus = jnp.roll(centre, -1, axis=-1)
    z_minus = jnp.roll(centre, 1, axis=-1)
    return (centre, x_plus, x_minus, y_plus, y_minus, z_plus, z_minus)


def operate(padded):
    centre, x_plus, x_minus, y_plus, y_minus, z_plus, z_minus = neighbours(padded)
    return (6.0 + SCREEN) * centre - (x_plus + x_minus + y_plus + y_minus + z_plus + z_minus)


def advect(padded):
    centre, x_plus, x_minus, y_plus, y_minus, z_plus, z_minus = neighbours(padded)
    laplace = x_plus + x_minus + y_plus + y_minus + z_plus + z_minus - 6.0 * centre
    transport = (
        centre[0:1] * (x_plus - x_minus) * 0.5
        + centre[1:2] * (y_plus - y_minus) * 0.5
        + centre[2:3] * (z_plus - z_minus) * 0.5
    )
    return centre + TIME_STEP * (VISCOSITY * laplace - transport)


def penalize(velocity, cell_swimmer, swimmer_speed):
    target = jnp.zeros_like(velocity)
    for swimmer in range(SWIMMERS):
        target = (
            target
            + (cell_swimmer == swimmer).astype(jnp.float32)[None]
            * swimmer_speed[swimmer][:, None, None, None]
        )
    solid = (cell_swimmer < SWIMMERS).astype(jnp.float32)[None]
    return (velocity + PENALTY * solid * target) / (1.0 + PENALTY * solid)


def divergence(flux_x, flux_y, flux_z):
    return (
        (flux_x[2:] - flux_x[:-2]) * 0.5
        + (flux_y[:, 2:] - flux_y[:, :-2]) * 0.5
        + (jnp.roll(flux_z, -1, axis=2) - jnp.roll(flux_z, 1, axis=2)) * 0.5
    )


def gradient(padded):
    centre, x_plus, x_minus, y_plus, y_minus, z_plus, z_minus = neighbours(padded)
    return jnp.stack([(x_plus - x_minus) * 0.5, (y_plus - y_minus) * 0.5, (z_plus - z_minus) * 0.5])


def plain(velocity, cell_swimmer, swimmer_speed, recentre_cols):
    width_x = velocity.shape[1]

    def search(_, state):
        pressure, residual = state
        extended = pad_walls(padded_2(residual, (("gx", 0), ("gy", 1)), 1, True), 1)
        image = operate(extended)
        norm_sq, curvature = lax.psum((jnp.sum(residual * residual), jnp.sum(residual * image)), AXES)
        alpha = norm_sq / curvature
        return (pressure + alpha * residual, residual - alpha * image)

    def step(step_index, state):
        velocity, _ = state
        offset = recentre_cols[step_index]
        tail_cols = velocity[:, width_x - SMAX :]
        received = shifted(tail_cols, "gx", 1)
        joined = jnp.concatenate([received, velocity], axis=1)
        velocity = lax.dynamic_slice_in_dim(joined, SMAX - offset, width_x, 1)
        padded = pad_walls(padded_2(velocity, (("gx", 1), ("gy", 2)), 1, True), 1)
        velocity = advect(padded)
        velocity = penalize(velocity, cell_swimmer, swimmer_speed)
        flux_x = padded_2(velocity[0], (("gx", 0),), 1, True)
        flux_y = padded_2(velocity[1], (("gy", 1),), 1, False)
        source = -divergence(flux_x, flux_y, velocity[2])
        pressure, _ = lax.fori_loop(0, PASSES, search, (jnp.zeros_like(source), source))
        padded = pad_walls(padded_2(pressure, (("gx", 0), ("gy", 1)), 1, True), 1)
        return (velocity - gradient(padded), pressure)

    start = (velocity, jnp.zeros(velocity.shape[1:], jnp.float32))
    return lax.fori_loop(0, STEPS, step, start)


def tables():
    angle = (np.arange(NODES) + 0.5) * np.pi / NODES
    cheb = np.cos(np.outer(np.arange(NODES), angle))
    moment = np.zeros((NODES, NODES))
    moment[0, 0] = moment[1, 1] = 1.0
    for i in range(1, NODES // 2):
        moment[2 * i, 2 * i], moment[2 * i, 0] = 2.0, -1.0
        moment[2 * i + 1, 2 * i + 1], moment[2 * i + 1, 1] = 2.0, -1.0
    scale = np.full((NODES, 1), 2.0 / NODES)
    scale[0] = 1.0 / NODES
    weight = cheb.T @ (scale * moment)
    weight_map = np.zeros((NODES, 128))
    weight_map[:, :NODES] = weight
    node = (6.0 + SCREEN) - 6.0 * np.cos(angle)
    node = np.broadcast_to(node[:, None], (NODES, NZ // 2))
    coef = np.broadcast_to((scale * cheb)[:PASSES, :, None], (PASSES, NODES, NZ // 2))
    return [np.ascontiguousarray(a, dtype=np.float32) for a in (weight_map, node, coef)]


HALF = NZ // 2


def halves(a):
    return a[:, :HALF], a[:, HALF:]


def z_pair(a, b):
    lane = lax.broadcasted_iota(jnp.int32, a.shape, 1)
    a_next, b_next = pltpu.roll(a, HALF - 1, 1), pltpu.roll(b, HALF - 1, 1)
    a_prev, b_prev = pltpu.roll(a, 1, 1), pltpu.roll(b, 1, 1)
    last, start = lane == HALF - 1, lane == 0
    return (
        (jnp.where(last, b_next, a_next), jnp.where(start, b_prev, a_prev)),
        (jnp.where(last, a_next, b_next), jnp.where(start, a_prev, b_prev)),
    )


def pack_kernel(velocity, cells, facing, along, theirs, mine):
    first = lax.axis_index("gx") % 2 == 0

    def put(i, plane, outputs):
        low, high = plane[0:8], plane[8:16]
        same, other = jnp.where(first, low, high), jnp.where(first, high, low)
        for out, value in zip(outputs, (same, other, same, other)):
            out[i] = value

    for i in range(4):
        for c in range(3):
            put(4 * c + i, velocity[c, i], (mine, theirs, along, facing))
        put(12 + i, cells[i].astype(jnp.float32), (mine, theirs))
    edge = jnp.where(first, cells[0], cells[3]).astype(jnp.float32)
    along[12] = jnp.where(first, edge[0:8], edge[8:16])
    facing[12] = jnp.where(first, edge[8:16], edge[0:8])


def source_kernel(
    info, flags, speed, left, own, right, from_core, from_chip, cell, cell_core, cell_chip, bodied, source, pad, ids, body, *, step
):
    core = info[0]
    joined = 2 - info[1 + step]
    up_flag, down_flag = flags[0], flags[1]

    def put(c, i, value):
        for h, part in enumerate(halves(value)):
            pad[c, i, h, 8:16] = part

    for c in range(3):
        for i in range(4):
            put(c, i, left[c, i])
        for i in range(8):
            put(c, i + 4, own[c, i])
        for i in range(2):
            put(c, i + 12, right[c, i])
        for i in range(1, 13):
            a, b = from_core[c, i - 1], from_chip[c, i - 1]
            up = jnp.where(core == 0, b, a) * up_flag
            down = jnp.where(core == 0, a, b) * down_flag
            for h in range(2):
                pad[c, i, h, 6:8] = halves(up)[h]
                pad[c, i, h, 16:18] = halves(down)[h]
    for i in range(10):
        a, b = cell_core[i], cell_chip[i]
        up, down = jnp.where(core == 0, b, a), jnp.where(core == 0, a, b)
        for h in range(2):
            ids[i, h, 8:16] = halves(cell[i])[h]
            ids[i, h, 6:8] = halves(up)[h]
            ids[i, h, 16:18] = halves(down)[h]

    row = lax.broadcasted_iota(jnp.int32, (8, HALF), 0)
    inside = (jnp.where(row == 0, up_flag, 1.0), jnp.where(row == 0, 1.0, down_flag))

    def move(i, _):
        p = i + 1 + joined
        for block in range(2):
            r = 7 + 8 * block
            centre = [[pad[c, p, h, r : r + 8] for h in range(2)] for c in range(3)]
            beside = [z_pair(*centre[c]) for c in range(3)]
            for h in range(2):
                cells = ids[i, h, r : r + 8]
                marks = [cells == swimmer for swimmer in range(SWIMMERS)]
                factor = jnp.where(cells < SWIMMERS, 1.0 / (1.0 + PENALTY), 1.0) * inside[block]
                for c in range(3):
                    here = centre[c][h]
                    x_plus, x_minus = pad[c, p + 1, h, r : r + 8], pad[c, p - 1, h, r : r + 8]
                    y_plus, y_minus = pad[c, p, h, r + 1 : r + 9], pad[c, p, h, r - 1 : r + 7]
                    z_plus, z_minus = beside[c][h]
                    laplace = x_plus + x_minus + y_plus + y_minus + z_plus + z_minus - 6.0 * here
                    transport = (
                        centre[0][h] * (x_plus - x_minus)
                        + centre[1][h] * (y_plus - y_minus)
                        + centre[2][h] * (z_plus - z_minus)
                    )
                    moved = here + (TIME_STEP * VISCOSITY) * laplace - (TIME_STEP * 0.5) * transport
                    target = jnp.zeros((8, HALF), jnp.float32)
                    for swimmer in range(SWIMMERS):
                        target = jnp.where(marks[swimmer], PENALTY * speed[swimmer, c], target)
                    body[c, i, h, 8 * block : 8 * block + 8] = (moved + target) * factor
        return 0

    for i in range(10):
        move(i, 0)

    for i in range(8):
        b2 = [body[2, i + 1, h, 1:9] for h in range(2)]
        beside = z_pair(*b2)
        for h in range(2):
            lanes = slice(h * HALF, (h + 1) * HALF)
            along_x = body[0, i + 2, h, 1:9] - body[0, i, h, 1:9]
            along_y = body[1, i + 1, h, 2:10] - body[1, i + 1, h, 0:8]
            along_z = beside[h][0] - beside[h][1]
            source[i, :, lanes] = -0.5 * (along_x + along_y + along_z)
            bodied[2, i, :, lanes] = b2[h]
            for c in range(2):
                bodied[c, i, :, lanes] = body[c, i + 1, h, 1:9]


def powers_kernel(info, flags, own, left, right, from_core, from_chip, moments, near, *t):
    core = info[0]
    scale = (flags[0], 1.0, flags[1])

    for i in range(24):
        k = min(max(i - 1, 0), 21)
        a, b = from_core[k], from_chip[k]
        up, down = jnp.where(core == 0, b, a) * scale[0], jnp.where(core == 0, a, b) * scale[2]
        middle = (left, own, right)[i // 8][i % 8]
        for h in range(2):
            t[0][i, h, 8:16] = halves(up)[h]
            t[0][i, h, 16:24] = halves(middle)[h]
            t[0][i, h, 24:32] = halves(down)[h]

    for j in range(1, PASSES + 1):
        blocks = (0, 1, 2) if j < PASSES else (1,)

        def level(i, _, j=j, blocks=blocks):
            for block in blocks:
                r = 8 + 8 * block
                factor = scale[block] * (1.0 / 6.0 if j == 1 else 1.0 / 3.0)
                beside = z_pair(t[j - 1][i, 0, r : r + 8], t[j - 1][i, 1, r : r + 8])
                for h in range(2):
                    total = (
                        (t[j - 1][i - 1, h, r : r + 8] + t[j - 1][i + 1, h, r : r + 8])
                        + (t[j - 1][i, h, r - 1 : r + 7] + t[j - 1][i, h, r + 1 : r + 9])
                        + (beside[h][0] + beside[h][1])
                    )
                    value = total * factor
                    if j > 1:
                        value = value - t[j - 2][i, h, r : r + 8]
                    t[j][i, h, r : r + 8] = value
            return 0

        for i in range(j, 24 - j):
            level(i, 0)

    def product(i, sums):
        out = list(sums)
        for h in range(2):
            values = [t[j][i, h, 16:24] for j in range(PASSES + 1)]
            for j in range(PASSES):
                out[2 * j] = out[2 * j] + values[j] * values[j]
                out[2 * j + 1] = out[2 * j + 1] + values[j] * values[j + 1]
        return tuple(out)

    zero = jnp.zeros((8, HALF), jnp.float32)
    sums = (zero,) * NODES
    for i in range(DEPTH, 2 * DEPTH):
        sums = product(i, sums)
    lines = [jnp.sum(a, axis=0, keepdims=True) for a in sums]
    block = jnp.concatenate(lines + [jnp.zeros((128 - NODES, 128), jnp.float32)], axis=0)
    line = jnp.sum(block.T, axis=0, keepdims=True)
    moments[...] = jnp.broadcast_to(line, moments.shape)

    def keep(i, _):
        for j in range(PASSES):
            for h in range(2):
                near[j, i, h, 0:8] = t[j][i + DEPTH - 1, h, 15:23]
                near[j, i, h, 8:16] = t[j][i + DEPTH - 1, h, 23:31]
        return 0

    for i in range(10):
        keep(i, 0)


def lengths(moments, weight_map, node, coef):
    line = jnp.sum(moments[...], axis=0, keepdims=True)
    weight = jnp.sum(weight_map[...] * line, axis=1, keepdims=True)
    weight = jnp.broadcast_to(weight, (NODES, HALF))
    first = jnp.sum(weight, axis=0, keepdims=True)
    value = node[...]
    residual = jnp.ones((NODES, HALF), jnp.float32)
    search = jnp.zeros((NODES, HALF), jnp.float32)
    good = jnp.ones((1, HALF), jnp.float32)
    for _ in range(PASSES):
        square = residual * residual
        norm_sq = jnp.sum(weight * square, axis=0, keepdims=True)
        curvature = jnp.sum(weight * square * value, axis=0, keepdims=True)
        noise = NOISE * first * jnp.sum(square, axis=0, keepdims=True)
        noise_image = NOISE * first * jnp.sum(square * value, axis=0, keepdims=True)
        good = jnp.where((norm_sq > noise) & (curvature > noise_image), good, 0.0)
        alpha = norm_sq / curvature
        search = search + alpha * residual
        residual = residual - alpha * value * residual
    terms = [jnp.sum(coef[j] * search, axis=0, keepdims=True) for j in range(PASSES)]
    return terms, good


def combine(terms, near, p):
    for i in range(10):
        for h in range(2):
            for r in (0, 8):
                total = terms[0] * near[0, i, h, r : r + 8]
                for j in range(1, PASSES):
                    total = total + terms[j] * near[j, i, h, r : r + 8]
                p[i, h, r : r + 8] = total


def corrected(i, bodied, p, put):
    own = [p[i + 1, h, 1:9] for h in range(2)]
    beside = z_pair(*own)
    for h in range(2):
        lanes = slice(h * HALF, (h + 1) * HALF)
        put(0, lanes, bodied[0, i, :, lanes] - 0.5 * (p[i + 2, h, 1:9] - p[i, h, 1:9]))
        put(1, lanes, bodied[1, i, :, lanes] - 0.5 * (p[i + 1, h, 2:10] - p[i + 1, h, 0:8]))
        put(2, lanes, bodied[2, i, :, lanes] - 0.5 * (beside[h][0] - beside[h][1]))
        put(3, lanes, own[h])


def inner_step_kernel(moments, weight_map, node, coef, near, bodied, good_out, velocity, p):
    terms, good = lengths(moments, weight_map, node, coef)
    good_out[...] = good
    combine(terms, near, p)
    for i in range(8):

        def put(c, lanes, value, i=i):
            if c < 3:
                velocity[c, i, :, lanes] = value

        corrected(i, bodied, p, put)


def last_step_kernel(info, moments, weight_map, node, coef, near, bodied, good_in, good_out, kept, sent, p):
    terms, good = lengths(moments, weight_map, node, coef)
    good_out[0] = (jnp.min(good * good_in[...]) > 0.5).astype(jnp.int32)
    core = info[0]
    combine(terms, near, p)
    for i in range(4):
        for out, start in ((sent, 4 * (1 - core)), (kept, 4 * core)):

            def put(c, lanes, value, i=i, out=out):
                out[c, i, :, lanes] = value

            corrected(start + i, bodied, p, put)


def place_kernel(info, kept, got, velocity, pressure):
    first = info[0] == 0
    for i in range(4):
        for c in range(4):
            a, b = kept[c, i], got[c, i]
            low, high = jnp.where(first, a, b), jnp.where(first, b, a)
            if c < 3:
                velocity[c, i, 0:8] = low
                velocity[c, i, 8:16] = high
            else:
                pressure[i, 0:8] = low
                pressure[i, 8:16] = high


SMEM = pl.BlockSpec(memory_space=pltpu.SMEM)
VMEM = pl.BlockSpec(memory_space=pltpu.VMEM)


def call(kernel, args, smem, outs, scratch, flags_out=0):
    specs, shapes = [VMEM] * len(outs), [jax.ShapeDtypeStruct(o, jnp.float32) for o in outs]
    if flags_out:
        specs, shapes = [SMEM] + specs, [jax.ShapeDtypeStruct((1,), jnp.int32)] + shapes
    return pl.pallas_call(
        kernel,
        in_specs=[SMEM] * smem + [VMEM] * (len(args) - smem),
        out_specs=specs,
        out_shape=shapes,
        scratch_shapes=[pltpu.VMEM(o, jnp.float32) for o in scratch],
        compiler_params=pltpu.CompilerParams(vmem_limit_bytes=24 * 1024 * 1024),
        cost_estimate=pl.CostEstimate(flops=1_000_000, bytes_accessed=1_000_000, transcendentals=0),
    )(*args)


def routes(count_x, count_y):
    chips = count_x // 2

    def pairs(target):
        out = []
        for chip in range(chips):
            for core in range(2):
                for y in range(count_y):
                    to = target(chip, core, y)
                    source = (2 * chip + core) * count_y + y
                    out.append((source, (2 * (to[0] % chips) + to[1]) * count_y + to[2]))
        return out

    def across(chip, core, y):
        return (chip, 1 - core, (y + (1 if core else -1)) % count_y)

    return {
        "core": pairs(lambda chip, core, y: (chip, 1 - core, y)),
        "facing": pairs(lambda chip, core, y: (chip + (1 if core else -1), 1 - core, y)),
        "along": pairs(lambda chip, core, y: (chip + (1 if core else -1), core, y)),
        "inner": pairs(lambda chip, core, y: (chip + (1 if chip % 2 == 0 else -1), core, y)),
        "outer": pairs(lambda chip, core, y: (chip + (-1 if chip % 2 == 0 else 1), core, y)),
        "across": pairs(across),
    }


def body(velocity, cell_swimmer, swimmer_speed, recentre_cols, *, count_x, count_y):
    route = routes(count_x, count_y)
    send = lambda value, name: lax.ppermute(value, AXES, route[name])
    core = lax.axis_index("gx") % 2
    y = lax.axis_index("gy")
    flags = jnp.stack([(y > 0) | (core == 1), (y < count_y - 1) | (core == 0)]).astype(jnp.float32)
    info = jnp.stack([core, recentre_cols[0], recentre_cols[1]]).astype(jnp.int32)
    weight_map, node, coef = (jnp.asarray(a) for a in tables())
    first = core == 0
    pick = lambda a, b: jnp.where(first, a, b)
    odd = (lax.axis_index("gx") // 2) % 2 == 1
    even = jnp.logical_not(odd)

    def beside(to_left, to_right, inner_first):
        inner = send(jnp.where(odd, to_left, to_right), "inner")
        outer = send(jnp.where(odd, to_right, to_left), "outer")
        if inner_first:
            return jnp.where(odd, inner, outer), jnp.where(odd, outer, inner)
        return jnp.where(even, outer, inner), jnp.where(even, inner, outer)


    facing, along, given, mine = call(
        pack_kernel, (velocity, cell_swimmer), 0, [(13, 8, NZ), (13, 8, NZ), (16, 8, NZ), (16, 8, NZ)], []
    )
    facing, theirs, along = send(facing, "facing"), send(given, "core"), send(along, "along")
    low, high = pick(mine, theirs), pick(theirs, mine)
    outer_low, outer_high = pick(facing, along), pick(along, facing)
    planes = lambda a: a[0:12].reshape(3, 4, 8, NZ)
    own = jnp.concatenate([planes(low), planes(high)], axis=1)
    left, right = planes(outer_low), planes(outer_high)[:, 0:2]
    cell = jnp.concatenate([outer_low[12:13], low[12:16], high[12:16], outer_high[12:13]], axis=0)

    for step in range(STEPS):
        if step:
            left, right = beside(own[:, 0:4], own[:, 4:8], False)
            right = right[:, 0:2]
        joined = jnp.concatenate([left, own, right], axis=1)
        if not step:
            spare = jnp.concatenate([cell[0:1], cell, cell[0:3]], axis=0)
            joined = jnp.concatenate([joined, spare[None]], axis=0)
        top, bottom = joined[:, 1:13, 0:2], joined[:, 1:13, 6:8]
        from_core, from_chip = send(pick(bottom, top), "core"), send(pick(top, bottom), "across")
        if not step:
            cell_core, cell_chip = from_core[3, 0:10], from_chip[3, 0:10]
        bodied, source = call(
            functools.partial(source_kernel, step=step),
            (info, flags, swimmer_speed, left, own, right, from_core, from_chip, cell, cell_core, cell_chip),
            3,
            [(3, 8, 8, NZ), (8, 8, NZ)],
            [(3, 14, 2, 24, HALF), (10, 2, 24, HALF), (3, 10, 2, 16, HALF)],
        )
        s_left, s_right = beside(source, source, step == 0)
        column = jnp.concatenate([s_left[1:], source, s_right[:7]], axis=0)
        moments, near = call(
            powers_kernel,
            (info, flags, source, s_left, s_right, send(column, "core"), send(column, "across")),
            2,
            [(count_x * count_y, 128), (PASSES, 10, 2, 16, HALF)],
            [(24, 2, 40, HALF)] * (PASSES + 1),
        )
        moments = lax.all_to_all(moments, AXES, 0, 0)
        shared = (moments, weight_map, node, coef, near, bodied)
        if step < STEPS - 1:
            good, own = call(inner_step_kernel, shared, 0, [(1, HALF), (3, 8, 8, NZ)], [(10, 2, 16, HALF)])
        else:
            good, kept, sent = call(
                last_step_kernel,
                (info,) + shared + (good,),
                1,
                [(4, 4, 8, NZ), (4, 4, 8, NZ)],
                [(10, 2, 16, HALF)],
                flags_out=1,
            )

    def finish(_):
        got = send(sent, "core")
        return tuple(call(place_kernel, (info, kept, got), 1, [(3, 4, 16, NZ), (4, 16, NZ)], []))

    def again(_):
        whole = jnp.concatenate([pick(mine, given), pick(given, mine)], axis=1)
        return plain(
            whole[0:12].reshape(3, 4, 16, NZ), whole[12:16].astype(jnp.int32), swimmer_speed, recentre_cols
        )

    return lax.cond(good[0] > 0, finish, again, None)


def solution(mesh):
    placed = (P(None, "gx", "gy", None), P("gx", "gy", None), P(), P())
    return jax.shard_map(
        functools.partial(body, count_x=mesh.shape["gx"], count_y=mesh.shape["gy"]),
        mesh=mesh,
        in_specs=placed,
        out_specs=(P(None, "gx", "gy", None), P("gx", "gy", None)),
        check_vma=False,
    )
```

```python
import functools

import jax
import jax.numpy as jnp
import numpy as np
from jax import lax
from jax.experimental import pallas as pl
from jax.experimental.pallas import tpu as pltpu
from jax.sharding import PartitionSpec as P

SWIMMERS = 8
STEPS = 2
PASSES = 8
SMAX = 2

TIME_STEP = 0.1
VISCOSITY = 0.5
PENALTY = 4.0
SCREEN = 0.05

AXES = ("gx", "gy")
NODES = 16
NZ = 256
DEPTH = 8
NOISE = 1e-5


def shifted(value, axis, steps):
    count = lax.axis_size(axis)
    pairs = [(source, (source + steps) % count) for source in range(count)]
    return lax.ppermute(value, axis, pairs)


def padded_2(cells, sides, width, closed):
    for axis, dim in sides:
        count = lax.axis_size(axis)
        ends = count if closed else count - 1
        head = lax.slice_in_dim(cells, 0, width, axis=dim)
        tail = lax.slice_in_dim(cells, cells.shape[dim] - width, cells.shape[dim], axis=dim)
        cells = jnp.concatenate(
            [
                lax.ppermute(tail, axis, [(i, (i + 1) % count) for i in range(ends)]),
                cells,
                lax.ppermute(head, axis, [((i + 1) % count, i) for i in range(ends)]),
            ],
            axis=dim,
        )
    return cells


def pad_walls(padded, width):
    row_count = padded.shape[-2]
    inner_rows = row_count - 2 * width
    global_rows = lax.axis_index("gy") * inner_rows + jnp.arange(row_count, dtype=jnp.int32) - width
    total_rows = inner_rows * lax.axis_size("gy")
    inside = ((global_rows >= 0) & (global_rows < total_rows)).astype(padded.dtype)
    return padded * inside[:, None]


def neighbours(padded):
    centre = padded[..., 1:-1, 1:-1, :]
    x_plus = padded[..., 2:, 1:-1, :]
    x_minus = padded[..., :-2, 1:-1, :]
    y_plus = padded[..., 1:-1, 2:, :]
    y_minus = padded[..., 1:-1, :-2, :]
    z_plus = jnp.roll(centre, -1, axis=-1)
    z_minus = jnp.roll(centre, 1, axis=-1)
    return (centre, x_plus, x_minus, y_plus, y_minus, z_plus, z_minus)


def operate(padded):
    centre, x_plus, x_minus, y_plus, y_minus, z_plus, z_minus = neighbours(padded)
    return (6.0 + SCREEN) * centre - (x_plus + x_minus + y_plus + y_minus + z_plus + z_minus)


def advect(padded):
    centre, x_plus, x_minus, y_plus, y_minus, z_plus, z_minus = neighbours(padded)
    laplace = x_plus + x_minus + y_plus + y_minus + z_plus + z_minus - 6.0 * centre
    transport = (
        centre[0:1] * (x_plus - x_minus) * 0.5
        + centre[1:2] * (y_plus - y_minus) * 0.5
        + centre[2:3] * (z_plus - z_minus) * 0.5
    )
    return centre + TIME_STEP * (VISCOSITY * laplace - transport)


def penalize(velocity, cell_swimmer, swimmer_speed):
    target = jnp.zeros_like(velocity)
    for swimmer in range(SWIMMERS):
        target = (
            target
            + (cell_swimmer == swimmer).astype(jnp.float32)[None]
            * swimmer_speed[swimmer][:, None, None, None]
        )
    solid = (cell_swimmer < SWIMMERS).astype(jnp.float32)[None]
    return (velocity + PENALTY * solid * target) / (1.0 + PENALTY * solid)


def divergence(flux_x, flux_y, flux_z):
    return (
        (flux_x[2:] - flux_x[:-2]) * 0.5
        + (flux_y[:, 2:] - flux_y[:, :-2]) * 0.5
        + (jnp.roll(flux_z, -1, axis=2) - jnp.roll(flux_z, 1, axis=2)) * 0.5
    )


def gradient(padded):
    centre, x_plus, x_minus, y_plus, y_minus, z_plus, z_minus = neighbours(padded)
    return jnp.stack([(x_plus - x_minus) * 0.5, (y_plus - y_minus) * 0.5, (z_plus - z_minus) * 0.5])


def plain(velocity, cell_swimmer, swimmer_speed, recentre_cols):
    width_x = velocity.shape[1]

    def search(_, state):
        pressure, residual = state
        extended = pad_walls(padded_2(residual, (("gx", 0), ("gy", 1)), 1, True), 1)
        image = operate(extended)
        norm_sq, curvature = lax.psum((jnp.sum(residual * residual), jnp.sum(residual * image)), AXES)
        alpha = norm_sq / curvature
        return (pressure + alpha * residual, residual - alpha * image)

    def step(step_index, state):
        velocity, _ = state
        offset = recentre_cols[step_index]
        tail_cols = velocity[:, width_x - SMAX :]
        received = shifted(tail_cols, "gx", 1)
        joined = jnp.concatenate([received, velocity], axis=1)
        velocity = lax.dynamic_slice_in_dim(joined, SMAX - offset, width_x, 1)
        padded = pad_walls(padded_2(velocity, (("gx", 1), ("gy", 2)), 1, True), 1)
        velocity = advect(padded)
        velocity = penalize(velocity, cell_swimmer, swimmer_speed)
        flux_x = padded_2(velocity[0], (("gx", 0),), 1, True)
        flux_y = padded_2(velocity[1], (("gy", 1),), 1, False)
        source = -divergence(flux_x, flux_y, velocity[2])
        pressure, _ = lax.fori_loop(0, PASSES, search, (jnp.zeros_like(source), source))
        padded = pad_walls(padded_2(pressure, (("gx", 0), ("gy", 1)), 1, True), 1)
        return (velocity - gradient(padded), pressure)

    start = (velocity, jnp.zeros(velocity.shape[1:], jnp.float32))
    return lax.fori_loop(0, STEPS, step, start)


def tables():
    angle = (np.arange(NODES) + 0.5) * np.pi / NODES
    cheb = np.cos(np.outer(np.arange(NODES), angle))
    moment = np.zeros((NODES, NODES))
    moment[0, 0] = moment[1, 1] = 1.0
    for i in range(1, NODES // 2):
        moment[2 * i, 2 * i], moment[2 * i, 0] = 2.0, -1.0
        moment[2 * i + 1, 2 * i + 1], moment[2 * i + 1, 1] = 2.0, -1.0
    scale = np.full((NODES, 1), 2.0 / NODES)
    scale[0] = 1.0 / NODES
    weight = cheb.T @ (scale * moment)
    weight_map = np.zeros((NODES, 128))
    weight_map[:, :NODES] = weight
    node = (6.0 + SCREEN) - 6.0 * np.cos(angle)
    node = np.broadcast_to(node[:, None], (NODES, NZ // 2))
    coef = np.broadcast_to((scale * cheb)[:PASSES, :, None], (PASSES, NODES, NZ // 2))
    return [np.ascontiguousarray(a, dtype=np.float32) for a in (weight_map, node, coef)]


HALF = NZ // 2


def halves(a):
    return a[:, :HALF], a[:, HALF:]


def z_pair(a, b):
    lane = lax.broadcasted_iota(jnp.int32, a.shape, 1)
    a_next, b_next = pltpu.roll(a, HALF - 1, 1), pltpu.roll(b, HALF - 1, 1)
    a_prev, b_prev = pltpu.roll(a, 1, 1), pltpu.roll(b, 1, 1)
    last, start = lane == HALF - 1, lane == 0
    return (
        (jnp.where(last, b_next, a_next), jnp.where(start, b_prev, a_prev)),
        (jnp.where(last, a_next, b_next), jnp.where(start, a_prev, b_prev)),
    )


def pack_kernel(velocity, cells, facing, along, theirs, mine):
    first = lax.axis_index("gx") % 2 == 0

    def put(i, plane, outputs):
        low, high = plane[0:8], plane[8:16]
        same, other = jnp.where(first, low, high), jnp.where(first, high, low)
        for out, value in zip(outputs, (same, other, same, other)):
            out[i] = value

    for i in range(4):
        for c in range(3):
            put(4 * c + i, velocity[c, i], (mine, theirs, along, facing))
        put(12 + i, cells[i].astype(jnp.float32), (mine, theirs))
    edge = jnp.where(first, cells[0], cells[3]).astype(jnp.float32)
    along[12] = jnp.where(first, edge[0:8], edge[8:16])
    facing[12] = jnp.where(first, edge[8:16], edge[0:8])


def source_kernel(
    info, flags, speed, left, own, right, from_core, from_chip, cell, cell_core, cell_chip, bodied, source, pad, ids, body, *, step
):
    core = info[0]
    joined = 2 - info[1 + step]
    up_flag, down_flag = flags[0], flags[1]

    def put(c, i, value):
        for h, part in enumerate(halves(value)):
            pad[c, i, h, 8:16] = part

    for c in range(3):
        for i in range(4):
            put(c, i, left[c, i])
        for i in range(8):
            put(c, i + 4, own[c, i])
        for i in range(2):
            put(c, i + 12, right[c, i])
        for i in range(1, 13):
            a, b = from_core[c, i - 1], from_chip[c, i - 1]
            up = jnp.where(core == 0, b, a) * up_flag
            down = jnp.where(core == 0, a, b) * down_flag
            for h in range(2):
                pad[c, i, h, 6:8] = halves(up)[h]
                pad[c, i, h, 16:18] = halves(down)[h]
    for i in range(10):
        a, b = cell_core[i], cell_chip[i]
        up, down = jnp.where(core == 0, b, a), jnp.where(core == 0, a, b)
        for h in range(2):
            ids[i, h, 8:16] = halves(cell[i])[h]
            ids[i, h, 6:8] = halves(up)[h]
            ids[i, h, 16:18] = halves(down)[h]

    row = lax.broadcasted_iota(jnp.int32, (8, HALF), 0)
    inside = (jnp.where(row == 0, up_flag, 1.0), jnp.where(row == 0, 1.0, down_flag))

    def move(i, _):
        p = i + 1 + joined
        for block in range(2):
            r = 7 + 8 * block
            centre = [[pad[c, p, h, r : r + 8] for h in range(2)] for c in range(3)]
            beside = [z_pair(*centre[c]) for c in range(3)]
            for h in range(2):
                cells = ids[i, h, r : r + 8]
                marks = [cells == swimmer for swimmer in range(SWIMMERS)]
                factor = jnp.where(cells < SWIMMERS, 1.0 / (1.0 + PENALTY), 1.0) * inside[block]
                for c in range(3):
                    here = centre[c][h]
                    x_plus, x_minus = pad[c, p + 1, h, r : r + 8], pad[c, p - 1, h, r : r + 8]
                    y_plus, y_minus = pad[c, p, h, r + 1 : r + 9], pad[c, p, h, r - 1 : r + 7]
                    z_plus, z_minus = beside[c][h]
                    laplace = x_plus + x_minus + y_plus + y_minus + z_plus + z_minus - 6.0 * here
                    transport = (
                        centre[0][h] * (x_plus - x_minus)
                        + centre[1][h] * (y_plus - y_minus)
                        + centre[2][h] * (z_plus - z_minus)
                    )
                    moved = here + (TIME_STEP * VISCOSITY) * laplace - (TIME_STEP * 0.5) * transport
                    target = jnp.zeros((8, HALF), jnp.float32)
                    for swimmer in range(SWIMMERS):
                        target = jnp.where(marks[swimmer], PENALTY * speed[swimmer, c], target)
                    body[c, i, h, 8 * block : 8 * block + 8] = (moved + target) * factor
        return 0

    for i in range(10):
        move(i, 0)

    for i in range(8):
        b2 = [body[2, i + 1, h, 1:9] for h in range(2)]
        beside = z_pair(*b2)
        for h in range(2):
            lanes = slice(h * HALF, (h + 1) * HALF)
            along_x = body[0, i + 2, h, 1:9] - body[0, i, h, 1:9]
            along_y = body[1, i + 1, h, 2:10] - body[1, i + 1, h, 0:8]
            along_z = beside[h][0] - beside[h][1]
            source[i, :, lanes] = -0.5 * (along_x + along_y + along_z)
            bodied[2, i, :, lanes] = b2[h]
            for c in range(2):
                bodied[c, i, :, lanes] = body[c, i + 1, h, 1:9]


def powers_kernel(info, flags, own, inner, outer, core_a, chip_a, core_b, chip_b, moments, near, *t):
    core = info[0]
    scale = (flags[0], 1.0, flags[1])

    odd = info[3] == 1

    def rows_beside(k, a, b):
        up = jnp.where(core == 0, b[k], a[k]) * scale[0]
        down = jnp.where(core == 0, a[k], b[k]) * scale[2]
        return up, down

    def put(i, up, middle, down):
        for h in range(2):
            t[0][i, h, 8:16] = halves(up)[h]
            t[0][i, h, 16:24] = halves(middle)[h]
            t[0][i, h, 24:32] = halves(down)[h]

    for i in range(8):
        up, down = rows_beside(i, core_a, chip_a)
        put(8 + i, up, own[i], down)
        k_left, k_right = max(i - 1, 0), min(i, 6)
        for plane, k, swap in ((i, k_left, odd), (16 + i, k_right, jnp.logical_not(odd))):
            near_rows = rows_beside(8 + k, core_a, chip_a)
            far_rows = rows_beside(k, core_b, chip_b)
            up, down = (jnp.where(swap, n, f) for n, f in zip(near_rows, far_rows))
            put(plane, up, jnp.where(swap, inner[i], outer[i]), down)

    for j in range(1, PASSES + 1):
        blocks = (0, 1, 2) if j < PASSES else (1,)

        def level(i, _, j=j, blocks=blocks):
            for block in blocks:
                r = 8 + 8 * block
                factor = scale[block] * (1.0 / 6.0 if j == 1 else 1.0 / 3.0)
                beside = z_pair(t[j - 1][i, 0, r : r + 8], t[j - 1][i, 1, r : r + 8])
                for h in range(2):
                    total = (
                        (t[j - 1][i - 1, h, r : r + 8] + t[j - 1][i + 1, h, r : r + 8])
                        + (t[j - 1][i, h, r - 1 : r + 7] + t[j - 1][i, h, r + 1 : r + 9])
                        + (beside[h][0] + beside[h][1])
                    )
                    value = total * factor
                    if j > 1:
                        value = value - t[j - 2][i, h, r : r + 8]
                    t[j][i, h, r : r + 8] = value
            return 0

        for i in range(j, 24 - j):
            level(i, 0)

    def product(i, sums):
        out = list(sums)
        for h in range(2):
            values = [t[j][i, h, 16:24] for j in range(PASSES + 1)]
            for j in range(PASSES):
                out[2 * j] = out[2 * j] + values[j] * values[j]
                out[2 * j + 1] = out[2 * j + 1] + values[j] * values[j + 1]
        return tuple(out)

    zero = jnp.zeros((8, HALF), jnp.float32)
    sums = (zero,) * NODES
    for i in range(DEPTH, 2 * DEPTH):
        sums = product(i, sums)
    lines = [jnp.sum(a, axis=0, keepdims=True) for a in sums]
    block = jnp.concatenate(lines + [jnp.zeros((128 - NODES, 128), jnp.float32)], axis=0)
    line = jnp.sum(block.T, axis=0, keepdims=True)
    moments[...] = jnp.broadcast_to(line, moments.shape)

    def keep(i, _):
        for j in range(PASSES):
            for h in range(2):
                near[j, i, h, 0:8] = t[j][i + DEPTH - 1, h, 15:23]
                near[j, i, h, 8:16] = t[j][i + DEPTH - 1, h, 23:31]
        return 0

    for i in range(10):
        keep(i, 0)


def lengths(moments, weight_map, node, coef):
    line = jnp.sum(moments[...], axis=0, keepdims=True)
    weight = jnp.sum(weight_map[...] * line, axis=1, keepdims=True)
    weight = jnp.broadcast_to(weight, (NODES, HALF))
    first = jnp.sum(weight, axis=0, keepdims=True)
    value = node[...]
    residual = jnp.ones((NODES, HALF), jnp.float32)
    search = jnp.zeros((NODES, HALF), jnp.float32)
    good = jnp.ones((1, HALF), jnp.float32)
    for _ in range(PASSES):
        square = residual * residual
        norm_sq = jnp.sum(weight * square, axis=0, keepdims=True)
        curvature = jnp.sum(weight * square * value, axis=0, keepdims=True)
        noise = NOISE * first * jnp.sum(square, axis=0, keepdims=True)
        noise_image = NOISE * first * jnp.sum(square * value, axis=0, keepdims=True)
        good = jnp.where((norm_sq > noise) & (curvature > noise_image), good, 0.0)
        alpha = norm_sq / curvature
        search = search + alpha * residual
        residual = residual - alpha * value * residual
    terms = [jnp.sum(coef[j] * search, axis=0, keepdims=True) for j in range(PASSES)]
    return terms, good


def combine(terms, near, p):
    for i in range(10):
        for h in range(2):
            for r in (0, 8):
                total = terms[0] * near[0, i, h, r : r + 8]
                for j in range(1, PASSES):
                    total = total + terms[j] * near[j, i, h, r : r + 8]
                p[i, h, r : r + 8] = total


def corrected(i, bodied, p, put):
    own = [p[i + 1, h, 1:9] for h in range(2)]
    beside = z_pair(*own)
    for h in range(2):
        lanes = slice(h * HALF, (h + 1) * HALF)
        put(0, lanes, bodied[0, i, :, lanes] - 0.5 * (p[i + 2, h, 1:9] - p[i, h, 1:9]))
        put(1, lanes, bodied[1, i, :, lanes] - 0.5 * (p[i + 1, h, 2:10] - p[i + 1, h, 0:8]))
        put(2, lanes, bodied[2, i, :, lanes] - 0.5 * (beside[h][0] - beside[h][1]))
        put(3, lanes, own[h])


def inner_step_kernel(moments, weight_map, node, coef, near, bodied, good_out, velocity, p):
    terms, good = lengths(moments, weight_map, node, coef)
    good_out[...] = good
    combine(terms, near, p)
    for i in range(8):

        def put(c, lanes, value, i=i):
            if c < 3:
                velocity[c, i, :, lanes] = value

        corrected(i, bodied, p, put)


def last_step_kernel(info, moments, weight_map, node, coef, near, bodied, good_in, good_out, kept, sent, p):
    terms, good = lengths(moments, weight_map, node, coef)
    good_out[0] = (jnp.min(good * good_in[...]) > 0.5).astype(jnp.int32)
    core = info[0]
    combine(terms, near, p)
    for i in range(4):
        for out, start in ((sent, 4 * (1 - core)), (kept, 4 * core)):

            def put(c, lanes, value, i=i, out=out):
                out[c, i, :, lanes] = value

            corrected(start + i, bodied, p, put)


def place_kernel(info, kept, got, velocity, pressure):
    first = info[0] == 0
    for i in range(4):
        for c in range(4):
            a, b = kept[c, i], got[c, i]
            low, high = jnp.where(first, a, b), jnp.where(first, b, a)
            if c < 3:
                velocity[c, i, 0:8] = low
                velocity[c, i, 8:16] = high
            else:
                pressure[i, 0:8] = low
                pressure[i, 8:16] = high


SMEM = pl.BlockSpec(memory_space=pltpu.SMEM)
VMEM = pl.BlockSpec(memory_space=pltpu.VMEM)


def call(kernel, args, smem, outs, scratch, flags_out=0):
    specs, shapes = [VMEM] * len(outs), [jax.ShapeDtypeStruct(o, jnp.float32) for o in outs]
    if flags_out:
        specs, shapes = [SMEM] + specs, [jax.ShapeDtypeStruct((1,), jnp.int32)] + shapes
    return pl.pallas_call(
        kernel,
        in_specs=[SMEM] * smem + [VMEM] * (len(args) - smem),
        out_specs=specs,
        out_shape=shapes,
        scratch_shapes=[pltpu.VMEM(o, jnp.float32) for o in scratch],
        compiler_params=pltpu.CompilerParams(vmem_limit_bytes=24 * 1024 * 1024),
        cost_estimate=pl.CostEstimate(flops=1_000_000, bytes_accessed=1_000_000, transcendentals=0),
    )(*args)


def routes(count_x, count_y):
    chips = count_x // 2

    def pairs(target):
        out = []
        for chip in range(chips):
            for core in range(2):
                for y in range(count_y):
                    to = target(chip, core, y)
                    source = (2 * chip + core) * count_y + y
                    out.append((source, (2 * (to[0] % chips) + to[1]) * count_y + to[2]))
        return out

    def across(chip, core, y):
        return (chip, 1 - core, (y + (1 if core else -1)) % count_y)

    return {
        "core": pairs(lambda chip, core, y: (chip, 1 - core, y)),
        "facing": pairs(lambda chip, core, y: (chip + (1 if core else -1), 1 - core, y)),
        "along": pairs(lambda chip, core, y: (chip + (1 if core else -1), core, y)),
        "inner": pairs(lambda chip, core, y: (chip + (1 if chip % 2 == 0 else -1), core, y)),
        "outer": pairs(lambda chip, core, y: (chip + (-1 if chip % 2 == 0 else 1), core, y)),
        "across": pairs(across),
    }


def body(velocity, cell_swimmer, swimmer_speed, recentre_cols, *, count_x, count_y):
    route = routes(count_x, count_y)
    send = lambda value, name: lax.ppermute(value, AXES, route[name])
    core = lax.axis_index("gx") % 2
    y = lax.axis_index("gy")
    flags = jnp.stack([(y > 0) | (core == 1), (y < count_y - 1) | (core == 0)]).astype(jnp.float32)
    info = jnp.stack([core, recentre_cols[0], recentre_cols[1], (lax.axis_index("gx") // 2) % 2]).astype(jnp.int32)
    weight_map, node, coef = (jnp.asarray(a) for a in tables())
    first = core == 0
    pick = lambda a, b: jnp.where(first, a, b)
    odd = (lax.axis_index("gx") // 2) % 2 == 1
    even = jnp.logical_not(odd)

    def beside(to_left, to_right, inner_first):
        inner = send(jnp.where(odd, to_left, to_right), "inner")
        outer = send(jnp.where(odd, to_right, to_left), "outer")
        if inner_first:
            return jnp.where(odd, inner, outer), jnp.where(odd, outer, inner)
        return jnp.where(even, outer, inner), jnp.where(even, inner, outer)


    facing, along, given, mine = call(
        pack_kernel, (velocity, cell_swimmer), 0, [(13, 8, NZ), (13, 8, NZ), (16, 8, NZ), (16, 8, NZ)], []
    )
    facing, theirs, along = send(facing, "facing"), send(given, "core"), send(along, "along")
    low, high = pick(mine, theirs), pick(theirs, mine)
    outer_low, outer_high = pick(facing, along), pick(along, facing)
    planes = lambda a: a[0:12].reshape(3, 4, 8, NZ)
    own = jnp.concatenate([planes(low), planes(high)], axis=1)
    left, right = planes(outer_low), planes(outer_high)[:, 0:2]
    cell = jnp.concatenate([outer_low[12:13], low[12:16], high[12:16], outer_high[12:13]], axis=0)

    for step in range(STEPS):
        if step:
            left, right = beside(own[:, 0:4], own[:, 4:8], False)
            right = right[:, 0:2]
        joined = jnp.concatenate([left, own, right], axis=1)
        if not step:
            spare = jnp.concatenate([cell[0:1], cell, cell[0:3]], axis=0)
            joined = jnp.concatenate([joined, spare[None]], axis=0)
        top, bottom = joined[:, 1:13, 0:2], joined[:, 1:13, 6:8]
        from_core, from_chip = send(pick(bottom, top), "core"), send(pick(top, bottom), "across")
        if not step:
            cell_core, cell_chip = from_core[3, 0:10], from_chip[3, 0:10]
        bodied, source = call(
            functools.partial(source_kernel, step=step),
            (info, flags, swimmer_speed, left, own, right, from_core, from_chip, cell, cell_core, cell_chip),
            3,
            [(3, 8, 8, NZ), (8, 8, NZ)],
            [(3, 14, 2, 24, HALF), (10, 2, 24, HALF), (3, 10, 2, 16, HALF)],
        )
        inner, outer = send(source, "inner"), send(source, "outer")
        early = jnp.concatenate([source, jnp.where(odd, inner[1:8], inner[0:7])], axis=0)
        early_core, early_chip = send(early, "core"), send(early, "across")
        late = jnp.where(odd, outer[0:7], outer[1:8])
        late_core, late_chip = send(late, "core"), send(late, "across")
        moments, near = call(
            powers_kernel,
            (info, flags, source, inner, outer, early_core, early_chip, late_core, late_chip),
            2,
            [(count_x * count_y, 128), (PASSES, 10, 2, 16, HALF)],
            [(24, 2, 40, HALF)] * (PASSES + 1),
        )
        moments = lax.all_to_all(moments, AXES, 0, 0)
        shared = (moments, weight_map, node, coef, near, bodied)
        if step < STEPS - 1:
            good, own = call(inner_step_kernel, shared, 0, [(1, HALF), (3, 8, 8, NZ)], [(10, 2, 16, HALF)])
        else:
            good, kept, sent = call(
                last_step_kernel,
                (info,) + shared + (good,),
                1,
                [(4, 4, 8, NZ), (4, 4, 8, NZ)],
                [(10, 2, 16, HALF)],
                flags_out=1,
            )

    def finish(_):
        got = send(sent, "core")
        return tuple(call(place_kernel, (info, kept, got), 1, [(3, 4, 16, NZ), (4, 16, NZ)], []))

    def again(_):
        whole = jnp.concatenate([pick(mine, given), pick(given, mine)], axis=1)
        return plain(
            whole[0:12].reshape(3, 4, 16, NZ), whole[12:16].astype(jnp.int32), swimmer_speed, recentre_cols
        )

    return lax.cond(good[0] > 0, finish, again, None)


def solution(mesh):
    placed = (P(None, "gx", "gy", None), P("gx", "gy", None), P(), P())
    return jax.shard_map(
        functools.partial(body, count_x=mesh.shape["gx"], count_y=mesh.shape["gy"]),
        mesh=mesh,
        in_specs=placed,
        out_specs=(P(None, "gx", "gy", None), P("gx", "gy", None)),
        check_vma=False,
    )
```

```python
import functools

import jax
import jax.numpy as jnp
import numpy as np
from jax import lax
from jax.experimental import pallas as pl
from jax.experimental.pallas import tpu as pltpu
from jax.sharding import PartitionSpec as P

SWIMMERS = 8
STEPS = 2
PASSES = 8
SMAX = 2

TIME_STEP = 0.1
VISCOSITY = 0.5
PENALTY = 4.0
SCREEN = 0.05

AXES = ("gx", "gy")
NODES = 16
NZ = 256
DEPTH = 8
NOISE = 1e-5


def shifted(value, axis, steps):
    count = lax.axis_size(axis)
    pairs = [(source, (source + steps) % count) for source in range(count)]
    return lax.ppermute(value, axis, pairs)


def padded_2(cells, sides, width, closed):
    for axis, dim in sides:
        count = lax.axis_size(axis)
        ends = count if closed else count - 1
        head = lax.slice_in_dim(cells, 0, width, axis=dim)
        tail = lax.slice_in_dim(cells, cells.shape[dim] - width, cells.shape[dim], axis=dim)
        cells = jnp.concatenate(
            [
                lax.ppermute(tail, axis, [(i, (i + 1) % count) for i in range(ends)]),
                cells,
                lax.ppermute(head, axis, [((i + 1) % count, i) for i in range(ends)]),
            ],
            axis=dim,
        )
    return cells


def pad_walls(padded, width):
    row_count = padded.shape[-2]
    inner_rows = row_count - 2 * width
    global_rows = lax.axis_index("gy") * inner_rows + jnp.arange(row_count, dtype=jnp.int32) - width
    total_rows = inner_rows * lax.axis_size("gy")
    inside = ((global_rows >= 0) & (global_rows < total_rows)).astype(padded.dtype)
    return padded * inside[:, None]


def neighbours(padded):
    centre = padded[..., 1:-1, 1:-1, :]
    x_plus = padded[..., 2:, 1:-1, :]
    x_minus = padded[..., :-2, 1:-1, :]
    y_plus = padded[..., 1:-1, 2:, :]
    y_minus = padded[..., 1:-1, :-2, :]
    z_plus = jnp.roll(centre, -1, axis=-1)
    z_minus = jnp.roll(centre, 1, axis=-1)
    return (centre, x_plus, x_minus, y_plus, y_minus, z_plus, z_minus)


def operate(padded):
    centre, x_plus, x_minus, y_plus, y_minus, z_plus, z_minus = neighbours(padded)
    return (6.0 + SCREEN) * centre - (x_plus + x_minus + y_plus + y_minus + z_plus + z_minus)


def advect(padded):
    centre, x_plus, x_minus, y_plus, y_minus, z_plus, z_minus = neighbours(padded)
    laplace = x_plus + x_minus + y_plus + y_minus + z_plus + z_minus - 6.0 * centre
    transport = (
        centre[0:1] * (x_plus - x_minus) * 0.5
        + centre[1:2] * (y_plus - y_minus) * 0.5
        + centre[2:3] * (z_plus - z_minus) * 0.5
    )
    return centre + TIME_STEP * (VISCOSITY * laplace - transport)


def penalize(velocity, cell_swimmer, swimmer_speed):
    target = jnp.zeros_like(velocity)
    for swimmer in range(SWIMMERS):
        target = (
            target
            + (cell_swimmer == swimmer).astype(jnp.float32)[None]
            * swimmer_speed[swimmer][:, None, None, None]
        )
    solid = (cell_swimmer < SWIMMERS).astype(jnp.float32)[None]
    return (velocity + PENALTY * solid * target) / (1.0 + PENALTY * solid)


def divergence(flux_x, flux_y, flux_z):
    return (
        (flux_x[2:] - flux_x[:-2]) * 0.5
        + (flux_y[:, 2:] - flux_y[:, :-2]) * 0.5
        + (jnp.roll(flux_z, -1, axis=2) - jnp.roll(flux_z, 1, axis=2)) * 0.5
    )


def gradient(padded):
    centre, x_plus, x_minus, y_plus, y_minus, z_plus, z_minus = neighbours(padded)
    return jnp.stack([(x_plus - x_minus) * 0.5, (y_plus - y_minus) * 0.5, (z_plus - z_minus) * 0.5])


def plain(velocity, cell_swimmer, swimmer_speed, recentre_cols):
    width_x = velocity.shape[1]

    def search(_, state):
        pressure, residual = state
        extended = pad_walls(padded_2(residual, (("gx", 0), ("gy", 1)), 1, True), 1)
        image = operate(extended)
        norm_sq, curvature = lax.psum((jnp.sum(residual * residual), jnp.sum(residual * image)), AXES)
        alpha = norm_sq / curvature
        return (pressure + alpha * residual, residual - alpha * image)

    def step(step_index, state):
        velocity, _ = state
        offset = recentre_cols[step_index]
        tail_cols = velocity[:, width_x - SMAX :]
        received = shifted(tail_cols, "gx", 1)
        joined = jnp.concatenate([received, velocity], axis=1)
        velocity = lax.dynamic_slice_in_dim(joined, SMAX - offset, width_x, 1)
        padded = pad_walls(padded_2(velocity, (("gx", 1), ("gy", 2)), 1, True), 1)
        velocity = advect(padded)
        velocity = penalize(velocity, cell_swimmer, swimmer_speed)
        flux_x = padded_2(velocity[0], (("gx", 0),), 1, True)
        flux_y = padded_2(velocity[1], (("gy", 1),), 1, False)
        source = -divergence(flux_x, flux_y, velocity[2])
        pressure, _ = lax.fori_loop(0, PASSES, search, (jnp.zeros_like(source), source))
        padded = pad_walls(padded_2(pressure, (("gx", 0), ("gy", 1)), 1, True), 1)
        return (velocity - gradient(padded), pressure)

    start = (velocity, jnp.zeros(velocity.shape[1:], jnp.float32))
    return lax.fori_loop(0, STEPS, step, start)


def tables():
    angle = (np.arange(NODES) + 0.5) * np.pi / NODES
    cheb = np.cos(np.outer(np.arange(NODES), angle))
    moment = np.zeros((NODES, NODES))
    moment[0, 0] = moment[1, 1] = 1.0
    for i in range(1, NODES // 2):
        moment[2 * i, 2 * i], moment[2 * i, 0] = 2.0, -1.0
        moment[2 * i + 1, 2 * i + 1], moment[2 * i + 1, 1] = 2.0, -1.0
    scale = np.full((NODES, 1), 2.0 / NODES)
    scale[0] = 1.0 / NODES
    weight = cheb.T @ (scale * moment)
    weight_map = np.zeros((NODES, 128))
    weight_map[:, :NODES] = weight
    node = (6.0 + SCREEN) - 6.0 * np.cos(angle)
    node = np.broadcast_to(node[:, None], (NODES, NZ // 2))
    coef = np.broadcast_to((scale * cheb)[:PASSES, :, None], (PASSES, NODES, NZ // 2))
    return [np.ascontiguousarray(a, dtype=np.float32) for a in (weight_map, node, coef)]


HALF = NZ // 2


def halves(a):
    return a[:, :HALF], a[:, HALF:]


def z_pair(a, b):
    lane = lax.broadcasted_iota(jnp.int32, a.shape, 1)
    a_next, b_next = pltpu.roll(a, HALF - 1, 1), pltpu.roll(b, HALF - 1, 1)
    a_prev, b_prev = pltpu.roll(a, 1, 1), pltpu.roll(b, 1, 1)
    last, start = lane == HALF - 1, lane == 0
    return (
        (jnp.where(last, b_next, a_next), jnp.where(start, b_prev, a_prev)),
        (jnp.where(last, a_next, b_next), jnp.where(start, a_prev, b_prev)),
    )


def pack_kernel(velocity, cells, facing, along, theirs, mine):
    first = lax.axis_index("gx") % 2 == 0

    def put(i, plane, outputs):
        low, high = plane[0:8], plane[8:16]
        same, other = jnp.where(first, low, high), jnp.where(first, high, low)
        for out, value in zip(outputs, (same, other, same, other)):
            out[i] = value

    for i in range(4):
        for c in range(3):
            put(4 * c + i, velocity[c, i], (mine, theirs, along, facing))
        put(12 + i, cells[i].astype(jnp.float32), (mine, theirs))
    edge = jnp.where(first, cells[0], cells[3]).astype(jnp.float32)
    along[12] = jnp.where(first, edge[0:8], edge[8:16])
    facing[12] = jnp.where(first, edge[8:16], edge[0:8])


def source_kernel(
    info, flags, speed, left, own, right, core_a, chip_a, core_b, chip_b, cell, cell_core, cell_chip, bodied, source, pad, ids, body, *, step
):
    core = info[0]
    joined = 2 - info[1 + step]
    up_flag, down_flag = flags[0], flags[1]

    def put(c, i, value):
        for h, part in enumerate(halves(value)):
            pad[c, i, h, 8:16] = part

    for c in range(3):
        for i in range(4):
            put(c, i, left[c, i])
        for i in range(8):
            put(c, i + 4, own[c, i])
        for i in range(2):
            put(c, i + 12, right[c, i])
        for i in range(1, 13):
            if 4 <= i < 12:
                a, b = core_a[c, i - 4], chip_a[c, i - 4]
            else:
                a, b = core_b[c, min(i - 1, 3)], chip_b[c, min(i - 1, 3)]
            up = jnp.where(core == 0, b, a) * up_flag
            down = jnp.where(core == 0, a, b) * down_flag
            for h in range(2):
                pad[c, i, h, 6:8] = halves(up)[h]
                pad[c, i, h, 16:18] = halves(down)[h]
    for i in range(10):
        a, b = cell_core[i], cell_chip[i]
        up, down = jnp.where(core == 0, b, a), jnp.where(core == 0, a, b)
        for h in range(2):
            ids[i, h, 8:16] = halves(cell[i])[h]
            ids[i, h, 6:8] = halves(up)[h]
            ids[i, h, 16:18] = halves(down)[h]

    row = lax.broadcasted_iota(jnp.int32, (8, HALF), 0)
    inside = (jnp.where(row == 0, up_flag, 1.0), jnp.where(row == 0, 1.0, down_flag))

    def move(i, _):
        p = i + 1 + joined
        for block in range(2):
            r = 7 + 8 * block
            centre = [[pad[c, p, h, r : r + 8] for h in range(2)] for c in range(3)]
            beside = [z_pair(*centre[c]) for c in range(3)]
            for h in range(2):
                cells = ids[i, h, r : r + 8]
                marks = [cells == swimmer for swimmer in range(SWIMMERS)]
                factor = jnp.where(cells < SWIMMERS, 1.0 / (1.0 + PENALTY), 1.0) * inside[block]
                for c in range(3):
                    here = centre[c][h]
                    x_plus, x_minus = pad[c, p + 1, h, r : r + 8], pad[c, p - 1, h, r : r + 8]
                    y_plus, y_minus = pad[c, p, h, r + 1 : r + 9], pad[c, p, h, r - 1 : r + 7]
                    z_plus, z_minus = beside[c][h]
                    laplace = x_plus + x_minus + y_plus + y_minus + z_plus + z_minus - 6.0 * here
                    transport = (
                        centre[0][h] * (x_plus - x_minus)
                        + centre[1][h] * (y_plus - y_minus)
                        + centre[2][h] * (z_plus - z_minus)
                    )
                    moved = here + (TIME_STEP * VISCOSITY) * laplace - (TIME_STEP * 0.5) * transport
                    target = jnp.zeros((8, HALF), jnp.float32)
                    for swimmer in range(SWIMMERS):
                        target = jnp.where(marks[swimmer], PENALTY * speed[swimmer, c], target)
                    body[c, i, h, 8 * block : 8 * block + 8] = (moved + target) * factor
        return 0

    for i in range(10):
        move(i, 0)

    for i in range(8):
        b2 = [body[2, i + 1, h, 1:9] for h in range(2)]
        beside = z_pair(*b2)
        for h in range(2):
            lanes = slice(h * HALF, (h + 1) * HALF)
            along_x = body[0, i + 2, h, 1:9] - body[0, i, h, 1:9]
            along_y = body[1, i + 1, h, 2:10] - body[1, i + 1, h, 0:8]
            along_z = beside[h][0] - beside[h][1]
            source[i, :, lanes] = -0.5 * (along_x + along_y + along_z)
            bodied[2, i, :, lanes] = b2[h]
            for c in range(2):
                bodied[c, i, :, lanes] = body[c, i + 1, h, 1:9]


def powers_kernel(info, flags, own, inner, outer, core_a, chip_a, core_b, chip_b, moments, near, *t):
    core = info[0]
    scale = (flags[0], 1.0, flags[1])

    odd = info[3] == 1

    def rows_beside(k, a, b):
        up = jnp.where(core == 0, b[k], a[k]) * scale[0]
        down = jnp.where(core == 0, a[k], b[k]) * scale[2]
        return up, down

    def put(i, up, middle, down):
        for h in range(2):
            t[0][i, h, 8:16] = halves(up)[h]
            t[0][i, h, 16:24] = halves(middle)[h]
            t[0][i, h, 24:32] = halves(down)[h]

    for i in range(8):
        up, down = rows_beside(i, core_a, chip_a)
        put(8 + i, up, own[i], down)
        k_left, k_right = max(i - 1, 0), min(i, 6)
        for plane, k, swap in ((i, k_left, odd), (16 + i, k_right, jnp.logical_not(odd))):
            near_rows = rows_beside(8 + k, core_a, chip_a)
            far_rows = rows_beside(k, core_b, chip_b)
            up, down = (jnp.where(swap, n, f) for n, f in zip(near_rows, far_rows))
            put(plane, up, jnp.where(swap, inner[i], outer[i]), down)

    for j in range(1, PASSES + 1):
        blocks = (0, 1, 2) if j < PASSES else (1,)

        def level(i, _, j=j, blocks=blocks):
            for block in blocks:
                r = 8 + 8 * block
                factor = scale[block] * (1.0 / 6.0 if j == 1 else 1.0 / 3.0)
                beside = z_pair(t[j - 1][i, 0, r : r + 8], t[j - 1][i, 1, r : r + 8])
                for h in range(2):
                    total = (
                        (t[j - 1][i - 1, h, r : r + 8] + t[j - 1][i + 1, h, r : r + 8])
                        + (t[j - 1][i, h, r - 1 : r + 7] + t[j - 1][i, h, r + 1 : r + 9])
                        + (beside[h][0] + beside[h][1])
                    )
                    value = total * factor
                    if j > 1:
                        value = value - t[j - 2][i, h, r : r + 8]
                    t[j][i, h, r : r + 8] = value
            return 0

        for i in range(j, 24 - j):
            level(i, 0)

    def product(i, sums):
        out = list(sums)
        for h in range(2):
            values = [t[j][i, h, 16:24] for j in range(PASSES + 1)]
            for j in range(PASSES):
                out[2 * j] = out[2 * j] + values[j] * values[j]
                out[2 * j + 1] = out[2 * j + 1] + values[j] * values[j + 1]
        return tuple(out)

    zero = jnp.zeros((8, HALF), jnp.float32)
    sums = (zero,) * NODES
    for i in range(DEPTH, 2 * DEPTH):
        sums = product(i, sums)
    lines = [jnp.sum(a, axis=0, keepdims=True) for a in sums]
    block = jnp.concatenate(lines + [jnp.zeros((128 - NODES, 128), jnp.float32)], axis=0)
    line = jnp.sum(block.T, axis=0, keepdims=True)
    moments[...] = jnp.broadcast_to(line, moments.shape)

    def keep(i, _):
        for j in range(PASSES):
            for h in range(2):
                near[j, i, h, 0:8] = t[j][i + DEPTH - 1, h, 15:23]
                near[j, i, h, 8:16] = t[j][i + DEPTH - 1, h, 23:31]
        return 0

    for i in range(10):
        keep(i, 0)


def lengths(moments, weight_map, node, coef):
    line = jnp.sum(moments[...], axis=0, keepdims=True)
    weight = jnp.sum(weight_map[...] * line, axis=1, keepdims=True)
    weight = jnp.broadcast_to(weight, (NODES, HALF))
    first = jnp.sum(weight, axis=0, keepdims=True)
    value = node[...]
    residual = jnp.ones((NODES, HALF), jnp.float32)
    search = jnp.zeros((NODES, HALF), jnp.float32)
    good = jnp.ones((1, HALF), jnp.float32)
    for _ in range(PASSES):
        square = residual * residual
        norm_sq = jnp.sum(weight * square, axis=0, keepdims=True)
        curvature = jnp.sum(weight * square * value, axis=0, keepdims=True)
        noise = NOISE * first * jnp.sum(square, axis=0, keepdims=True)
        noise_image = NOISE * first * jnp.sum(square * value, axis=0, keepdims=True)
        good = jnp.where((norm_sq > noise) & (curvature > noise_image), good, 0.0)
        alpha = norm_sq / curvature
        search = search + alpha * residual
        residual = residual - alpha * value * residual
    terms = [jnp.sum(coef[j] * search, axis=0, keepdims=True) for j in range(PASSES)]
    return terms, good


def combine(terms, near, p):
    for i in range(10):
        for h in range(2):
            for r in (0, 8):
                total = terms[0] * near[0, i, h, r : r + 8]
                for j in range(1, PASSES):
                    total = total + terms[j] * near[j, i, h, r : r + 8]
                p[i, h, r : r + 8] = total


def corrected(i, bodied, p, put):
    own = [p[i + 1, h, 1:9] for h in range(2)]
    beside = z_pair(*own)
    for h in range(2):
        lanes = slice(h * HALF, (h + 1) * HALF)
        put(0, lanes, bodied[0, i, :, lanes] - 0.5 * (p[i + 2, h, 1:9] - p[i, h, 1:9]))
        put(1, lanes, bodied[1, i, :, lanes] - 0.5 * (p[i + 1, h, 2:10] - p[i + 1, h, 0:8]))
        put(2, lanes, bodied[2, i, :, lanes] - 0.5 * (beside[h][0] - beside[h][1]))
        put(3, lanes, own[h])


def inner_step_kernel(moments, weight_map, node, coef, near, bodied, good_out, velocity, p):
    terms, good = lengths(moments, weight_map, node, coef)
    good_out[...] = good
    combine(terms, near, p)
    for i in range(8):

        def put(c, lanes, value, i=i):
            if c < 3:
                velocity[c, i, :, lanes] = value

        corrected(i, bodied, p, put)


def last_step_kernel(info, moments, weight_map, node, coef, near, bodied, good_in, good_out, kept, sent, p):
    terms, good = lengths(moments, weight_map, node, coef)
    good_out[0] = (jnp.min(good * good_in[...]) > 0.5).astype(jnp.int32)
    core = info[0]
    combine(terms, near, p)
    for i in range(4):
        for out, start in ((sent, 4 * (1 - core)), (kept, 4 * core)):

            def put(c, lanes, value, i=i, out=out):
                out[c, i, :, lanes] = value

            corrected(start + i, bodied, p, put)


def place_kernel(info, kept, got, velocity, pressure):
    first = info[0] == 0
    for i in range(4):
        for c in range(4):
            a, b = kept[c, i], got[c, i]
            low, high = jnp.where(first, a, b), jnp.where(first, b, a)
            if c < 3:
                velocity[c, i, 0:8] = low
                velocity[c, i, 8:16] = high
            else:
                pressure[i, 0:8] = low
                pressure[i, 8:16] = high


SMEM = pl.BlockSpec(memory_space=pltpu.SMEM)
VMEM = pl.BlockSpec(memory_space=pltpu.VMEM)


def call(kernel, args, smem, outs, scratch, flags_out=0):
    specs, shapes = [VMEM] * len(outs), [jax.ShapeDtypeStruct(o, jnp.float32) for o in outs]
    if flags_out:
        specs, shapes = [SMEM] + specs, [jax.ShapeDtypeStruct((1,), jnp.int32)] + shapes
    return pl.pallas_call(
        kernel,
        in_specs=[SMEM] * smem + [VMEM] * (len(args) - smem),
        out_specs=specs,
        out_shape=shapes,
        scratch_shapes=[pltpu.VMEM(o, jnp.float32) for o in scratch],
        compiler_params=pltpu.CompilerParams(vmem_limit_bytes=24 * 1024 * 1024),
        cost_estimate=pl.CostEstimate(flops=1_000_000, bytes_accessed=1_000_000, transcendentals=0),
    )(*args)


def routes(count_x, count_y):
    chips = count_x // 2

    def pairs(target):
        out = []
        for chip in range(chips):
            for core in range(2):
                for y in range(count_y):
                    to = target(chip, core, y)
                    source = (2 * chip + core) * count_y + y
                    out.append((source, (2 * (to[0] % chips) + to[1]) * count_y + to[2]))
        return out

    def across(chip, core, y):
        return (chip, 1 - core, (y + (1 if core else -1)) % count_y)

    return {
        "core": pairs(lambda chip, core, y: (chip, 1 - core, y)),
        "facing": pairs(lambda chip, core, y: (chip + (1 if core else -1), 1 - core, y)),
        "along": pairs(lambda chip, core, y: (chip + (1 if core else -1), core, y)),
        "inner": pairs(lambda chip, core, y: (chip + (1 if chip % 2 == 0 else -1), core, y)),
        "outer": pairs(lambda chip, core, y: (chip + (-1 if chip % 2 == 0 else 1), core, y)),
        "across": pairs(across),
    }


def body(velocity, cell_swimmer, swimmer_speed, recentre_cols, *, count_x, count_y):
    route = routes(count_x, count_y)
    send = lambda value, name: lax.ppermute(value, AXES, route[name])
    core = lax.axis_index("gx") % 2
    y = lax.axis_index("gy")
    flags = jnp.stack([(y > 0) | (core == 1), (y < count_y - 1) | (core == 0)]).astype(jnp.float32)
    info = jnp.stack([core, recentre_cols[0], recentre_cols[1], (lax.axis_index("gx") // 2) % 2]).astype(jnp.int32)
    weight_map, node, coef = (jnp.asarray(a) for a in tables())
    first = core == 0
    pick = lambda a, b: jnp.where(first, a, b)
    odd = (lax.axis_index("gx") // 2) % 2 == 1
    even = jnp.logical_not(odd)

    def beside(to_left, to_right, inner_first):
        inner = send(jnp.where(odd, to_left, to_right), "inner")
        outer = send(jnp.where(odd, to_right, to_left), "outer")
        if inner_first:
            return jnp.where(odd, inner, outer), jnp.where(odd, outer, inner)
        return jnp.where(even, outer, inner), jnp.where(even, inner, outer)


    facing, along, given, mine = call(
        pack_kernel, (velocity, cell_swimmer), 0, [(13, 8, NZ), (13, 8, NZ), (16, 8, NZ), (16, 8, NZ)], []
    )
    facing, theirs, along = send(facing, "facing"), send(given, "core"), send(along, "along")
    low, high = pick(mine, theirs), pick(theirs, mine)
    outer_low, outer_high = pick(facing, along), pick(along, facing)
    planes = lambda a: a[0:12].reshape(3, 4, 8, NZ)
    own = jnp.concatenate([planes(low), planes(high)], axis=1)
    left, right = planes(outer_low), planes(outer_high)[:, 0:2]
    cell = jnp.concatenate([outer_low[12:13], low[12:16], high[12:16], outer_high[12:13]], axis=0)

    for step in range(STEPS):
        if step:
            left, right = beside(own[:, 0:4], own[:, 4:8], False)
            right = right[:, 0:2]
        near_planes, far_planes = own, jnp.concatenate([left[:, 1:4], right[:, 0:1]], axis=1)
        if not step:
            near_planes = jnp.concatenate([own, jnp.concatenate([cell[3:10], cell[9:10]], axis=0)[None]], axis=0)
            far_planes = jnp.concatenate([far_planes, jnp.concatenate([cell[0:3], cell[2:3]], axis=0)[None]], axis=0)
        edges = []
        for planes_out in (near_planes, far_planes):
            top, bottom = planes_out[:, :, 0:2], planes_out[:, :, 6:8]
            edges += [send(pick(bottom, top), "core"), send(pick(top, bottom), "across")]
        if not step:
            cell_core = jnp.concatenate([edges[2][3, 0:3], edges[0][3, 0:7]], axis=0)
            cell_chip = jnp.concatenate([edges[3][3, 0:3], edges[1][3, 0:7]], axis=0)
        bodied, source = call(
            functools.partial(source_kernel, step=step),
            (info, flags, swimmer_speed, left, own, right, *edges, cell, cell_core, cell_chip),
            3,
            [(3, 8, 8, NZ), (8, 8, NZ)],
            [(3, 14, 2, 24, HALF), (10, 2, 24, HALF), (3, 10, 2, 16, HALF)],
        )
        inner, outer = send(source, "inner"), send(source, "outer")
        early = jnp.concatenate([source, jnp.where(odd, inner[1:8], inner[0:7])], axis=0)
        early_core, early_chip = send(early, "core"), send(early, "across")
        late = jnp.where(odd, outer[0:7], outer[1:8])
        late_core, late_chip = send(late, "core"), send(late, "across")
        moments, near = call(
            powers_kernel,
            (info, flags, source, inner, outer, early_core, early_chip, late_core, late_chip),
            2,
            [(count_x * count_y, 128), (PASSES, 10, 2, 16, HALF)],
            [(24, 2, 40, HALF)] * (PASSES + 1),
        )
        moments = lax.all_to_all(moments, AXES, 0, 0)
        shared = (moments, weight_map, node, coef, near, bodied)
        if step < STEPS - 1:
            good, own = call(inner_step_kernel, shared, 0, [(1, HALF), (3, 8, 8, NZ)], [(10, 2, 16, HALF)])
        else:
            good, kept, sent = call(
                last_step_kernel,
                (info,) + shared + (good,),
                1,
                [(4, 4, 8, NZ), (4, 4, 8, NZ)],
                [(10, 2, 16, HALF)],
                flags_out=1,
            )

    def finish(_):
        got = send(sent, "core")
        return tuple(call(place_kernel, (info, kept, got), 1, [(3, 4, 16, NZ), (4, 16, NZ)], []))

    def again(_):
        whole = jnp.concatenate([pick(mine, given), pick(given, mine)], axis=1)
        return plain(
            whole[0:12].reshape(3, 4, 16, NZ), whole[12:16].astype(jnp.int32), swimmer_speed, recentre_cols
        )

    return lax.cond(good[0] > 0, finish, again, None)


def solution(mesh):
    placed = (P(None, "gx", "gy", None), P("gx", "gy", None), P(), P())
    return jax.shard_map(
        functools.partial(body, count_x=mesh.shape["gx"], count_y=mesh.shape["gy"]),
        mesh=mesh,
        in_specs=placed,
        out_specs=(P(None, "gx", "gy", None), P("gx", "gy", None)),
        check_vma=False,
    )
```
